256 devices in a mesh: section: 2 (over core), row: 16 (over y_hi, z), hid: 8 (over y_lo, x).
Axes of the slice: x: 4, y: 4 (y_hi: 2, y_lo: 2; y = y_hi * 2 + y_lo), z: 8, core: 2. Of those that a mesh axis runs over, the one named last changes fastest.
Arguments:
- cotangent: bfloat16 [2048, 8192], P(None, 'row'), may hold values from -6 to 6
- pre_activation: bfloat16 [2048, 32768], P('row', ('section', 'hid')), may hold values from -6 to 6
- up_weight: bfloat16 [8192, 32768], P('row', ('section', 'hid')), may hold values from -0.0625 to 0.0625
- down_weight: bfloat16 [32768, 8192], P(('section', 'hid'), 'row'), may hold values from -0.03125 to 0.03125
- out_weight: bfloat16 [8192, 8192], P(('section', 'hid'), 'row'), may hold values from -0.0625 to 0.0625
Outputs:
- attn_grad: bfloat16 [2048, 8192], P('row', ('section', 'hid'))
The draws below stay inside these ranges and needn't reach their ends.
All inputs are finite; a program needn't handle non-finite values.
Results may differ from the reference program's by a relative error of at most 0.024.
Values may be sent and summed in bfloat16 or wider, within the bound.
No kernel may reach another device: no remote copies, remote signals or barrier semaphores. Data moves between devices by JAX's collectives and lax.ppermute only.
A program may use at most 64 MiB of HBM per device.

```python
import jax
import jax.numpy as jnp
from jax import lax

D = 8192
FF = 32768
TOKENS = 2048
N_SECTION = 2
N_ROW = 16
N_HID = 8


def steps_of(own_key, dims, split, smallest, high):
    gain, own = 1.0, jax.random.fold_in(own_key, 6)
    for position, blocks in split:
        steps = jnp.exp(jax.random.uniform(jax.random.fold_in(own, position), (blocks,), jnp.float32, smallest / len(split), high / len(split)))
        gain = gain * jnp.repeat(steps, dims[position] // blocks).reshape([-1 if axis == position else 1 for axis in range(len(dims))])
    return gain


def bell_draw(rng, shape, deviation, limit, pieces=(), kind=jnp.bfloat16):
    gain = steps_of(rng, shape, pieces, -0.22, 0.18) if pieces else 1.0
    drawn = jax.random.normal(rng, shape, jnp.float32) * deviation * gain
    return jnp.minimum(jnp.maximum(drawn, -limit), limit).astype(kind)


def setup_inputs(seed: int = 0) -> dict:
    key_list = jax.random.split(jax.random.key(seed), 6)
    return {
        "cotangent": bell_draw(key_list[0], (TOKENS, D), 1.0, 6.0, ((1, 16),)),
        "pre_activation": bell_draw(key_list[1], (TOKENS, FF), 1.0, 6.0, ((0, 16), (1, 16))),
        "up_weight": bell_draw(key_list[2], (D, FF), D ** -0.5, 0.0625, ((0, 16), (1, 16))),
        "down_weight": bell_draw(key_list[3], (FF, D), FF ** -0.5, 0.03125, ((0, 16), (1, 16))),
        "out_weight": bell_draw(key_list[4], (D, D), D ** -0.5, 0.0625, ((0, 16), (1, 16))),
    }


def gelu_slope(value):
    inner = 0.7978845608 * (value + 0.044715 * value * value * value)
    tanh_part = jnp.tanh(inner)
    derivative = 0.7978845608 * (1.0 + 3.0 * 0.044715 * value * value)
    return 0.5 * (1.0 + tanh_part) + 0.5 * value * (1.0 - tanh_part * tanh_part) * derivative


def rounded(value):
    return lax.optimization_barrier(value.astype(jnp.bfloat16)).astype(jnp.float32)


def reference(cotangent, pre_activation, up_weight, down_weight, out_weight):
    feat_block = D // N_ROW
    unit_block = FF // (N_SECTION * N_HID)
    hidden_grad = jnp.zeros((TOKENS, FF), jnp.float32)
    for block in range(N_ROW):
        lower = block * feat_block
        partial_term = jnp.dot(cotangent[:, lower:lower + feat_block], down_weight[:, lower:lower + feat_block].T, preferred_element_type=jnp.float32)
        hidden_grad = hidden_grad + rounded(partial_term)
    pre_grad = (hidden_grad * gelu_slope(pre_activation.astype(jnp.float32))).astype(jnp.bfloat16)
    total = cotangent.astype(jnp.float32)
    for block in range(N_SECTION * N_HID):
        lower = block * unit_block
        partial_term = jnp.dot(pre_grad[:, lower:lower + unit_block], up_weight[:, lower:lower + unit_block].T, preferred_element_type=jnp.float32)
        total = total + rounded(partial_term)
    input_grad = total.astype(jnp.bfloat16)
    result = jnp.zeros((TOKENS, D), jnp.float32)
    for block in range(N_ROW):
        lower = block * feat_block
        partial_term = jnp.dot(input_grad[:, lower:lower + feat_block], out_weight[:, lower:lower + feat_block].T, preferred_element_type=jnp.float32)
        result = result + rounded(partial_term)
    return result.astype(jnp.bfloat16)
```

```python
import jax
import jax.numpy as jnp
from jax import lax
from jax.sharding import Mesh, PartitionSpec as P

N_Z = 8
N_X = 4
AXES = ("section", "y_hi", "z", "y_lo", "x")
ROW = ("y_hi", "z")
COLUMN = ("section", "y_lo", "x")
BF16 = jnp.bfloat16
F32 = jnp.float32
NEAR, FAR = (0, 1, -1, 2, -2), (3, -3, 4)


def gelu_slope(value):
    inner = 0.7978845608 * (value + 0.044715 * value * value * value)
    tanh_part = jnp.tanh(inner)
    derivative = 0.7978845608 * (1.0 + 3.0 * 0.044715 * value * value)
    return 0.5 * (1.0 + tanh_part) + 0.5 * value * (1.0 - tanh_part * tanh_part) * derivative


def times_transposed(left, right):
    return lax.dot_general(
        left, right, (((1,), (1,)), ((), ())), preferred_element_type=F32
    )


def move(value, where):
    pairs = []
    for core in range(2):
        for y_hi in range(2):
            for z in range(N_Z):
                for y_lo in range(2):
                    for x in range(N_X):
                        c, h, k, l, i = where(core, y_hi, z, y_lo, x)
                        source = ((core * 2 + y_hi) * N_Z + z) * 2 * N_X + y_lo * N_X + x
                        target = ((c * 2 + h) * N_Z + k % N_Z) * 2 * N_X + l * N_X + i % N_X
                        pairs.append((source, target))
    return lax.ppermute(value, AXES, pairs)


def to_other_core(value):
    return move(value, lambda c, h, z, l, x: (1 - c, h, z, l, x))


def to_y_hi(value):
    return move(value, lambda c, h, z, l, x: (c, 1 - h, z, l, x))


def to_swapped(value):
    return move(value, lambda c, h, z, l, x: (h, c, z, l, x))


def along_z(value, sign):
    return move(value, lambda c, h, z, l, x: (c, h, z + (sign if c == 0 else -sign), l, x))


def added(*terms):
    total = terms[0].astype(F32)
    for term in terms[1:]:
        total = total + term.astype(F32)
    return total


def after(value, *others):
    return lax.optimization_barrier((value, *others))[0]


class Scatter:
    def __init__(self, part, offset=0):
        self.part, self.left, self.offset = part, 4, offset
        self.ahead = self.back = None

    def step(self, *waits):
        mine = self.part(self.left)
        behind = 1 - self.offset - self.left
        far = self.part(behind) if -4 < behind < 0 else None
        if self.ahead is not None:
            mine = added(mine, self.ahead).astype(BF16)
        if self.back is not None and far is not None:
            far = added(far, self.back).astype(BF16)
        if far is not None:
            mine, far = lax.optimization_barrier((mine, far, *waits))[:2]
        elif waits:
            mine = after(mine, *waits)
        self.ahead = along_z(mine, 1)
        if far is not None:
            self.back = along_z(far, -1)
        self.left -= 1
        return self.arrived()

    def arrived(self):
        return [self.ahead, self.back]

    def result(self):
        return added(self.part(0), self.ahead, self.back)


class Gather:
    def __init__(self, block):
        self.blocks, self.distance = {0: block}, 0
        self.ahead = self.back = block

    def step(self, *waits):
        self.distance += 1
        ahead, back = lax.optimization_barrier((self.ahead, self.back, *waits))[:2]
        self.ahead = along_z(ahead, 1)
        self.blocks[4 if self.distance == 4 else -self.distance] = self.ahead
        if self.distance < 4:
            self.back = along_z(back, -1)
            self.blocks[self.distance] = self.back
        return [self.ahead, self.back]


def body(cotangent, pre_activation, up_weight, down_weight, out_weight):
    tokens, feats = cotangent.shape
    half_tokens = tokens // 2
    rows = half_tokens // N_Z
    early = down_weight.shape[0] // 2
    part_units = early // 2
    pieces = 4 * N_X
    core = lax.axis_index("section")
    y_hi = lax.axis_index("y_hi")
    z = lax.axis_index("z")
    y_lo = lax.axis_index("y_lo")
    x = lax.axis_index("x")
    way = 1 - 2 * core

    def block_start(distance):
        return ((z + way * distance + N_Z) % N_Z) * rows

    def half_of(array, index, axis):
        size = array.shape[axis] // 2
        return lax.dynamic_slice_in_dim(array, index * size, size, axis)

    def early_of(array, index, axis):
        return lax.dynamic_slice_in_dim(array, index * part_units, part_units, axis)

    def late_of(array, index, axis):
        return lax.dynamic_slice_in_dim(array, early + index * part_units, part_units, axis)

    def both_of(array, index, axis):
        return jnp.concatenate([early_of(array, index, axis), late_of(array, index, axis)], axis=axis)

    def rows_of(product):
        return lambda distance: lax.dynamic_slice_in_dim(product, block_start(distance), rows, 0)

    cot = half_of(cotangent, core, 0)
    down_other = to_other_core(down_weight[:early])
    theirs = to_y_hi(jnp.concatenate([late_of(down_weight, 1 - y_hi, 0), cot], axis=0))

    own_ring = Scatter(rows_of(times_transposed(cot, down_weight[:early]).astype(BF16)))
    other_product = times_transposed(cot, down_other).astype(BF16)
    other_ring = Scatter(rows_of(other_product))
    own_first = own_ring.step()
    other_first = other_ring.step()

    late_mine = late_of(down_weight, y_hi, 0)
    late_mine_other = to_other_core(after(late_mine, *own_first))

    theirs = after(theirs, *other_first)
    late_theirs, cot_theirs = theirs[:part_units], theirs[part_units:]
    late_theirs_other = to_other_core(late_theirs)
    own_second = own_ring.step(other_product)
    other_second = other_ring.step(*own_first)
    late_mine = jnp.concatenate([late_mine, late_mine_other], axis=0)
    late_far = jnp.concatenate([late_theirs, late_theirs_other], axis=0)
    late_product = (
        times_transposed(cot, late_mine) + times_transposed(cot_theirs, late_far)
    ).astype(BF16)
    own_third = own_ring.step(*other_first)
    late_ring = Scatter(rows_of(late_product))
    other_third = other_ring.step(*own_second, late_product)
    late_first = late_ring.step()
    own_fourth = own_ring.step(*other_second)
    late_second = late_ring.step(*own_third)
    other_ring.step(*own_third, *late_first)
    late_ring.step(*other_third)

    act = after(pre_activation, theirs)
    act_first = to_swapped(both_of(act, core, 1))
    act_second = move(both_of(act, 1 - core, 1), lambda c, h, z, l, x: (h, 1 - c, z, l, x))
    act_first, act_second = after(act_first, *late_second), after(act_second, *late_second)

    straight = core == y_hi
    slope_own = gelu_slope(jnp.where(straight, act_first, act_second).astype(F32))
    slope_other = gelu_slope(jnp.where(straight, act_second, act_first).astype(F32))
    slope_early = jnp.concatenate([slope_own[:, :part_units], slope_other[:, :part_units]], axis=1)
    slope_late = jnp.concatenate([slope_own[:, part_units:], slope_other[:, part_units:]], axis=1)
    own_sums, other_sums = own_ring.result(), other_ring.result()

    def split_sums(index):
        return jnp.concatenate([early_of(own_sums, index, 1), early_of(other_sums, index, 1)], axis=1)

    early_arrived = to_y_hi(split_sums(1 - y_hi).astype(BF16))
    early_sums = added(split_sums(y_hi), early_arrived)
    first_ring = Gather((early_sums * slope_early).astype(BF16))
    late_fourth = late_ring.step(*own_fourth)
    second_ring = Gather((late_ring.result() * slope_late).astype(BF16))

    up = after(up_weight, early_arrived)
    up_mine = both_of(up, y_hi, 1)
    up_theirs = after(to_y_hi(both_of(up, 1 - y_hi, 1)), *late_fourth)
    up_own = jnp.concatenate(
        [jnp.where(y_hi == 0, up_mine, up_theirs), jnp.where(y_hi == 0, up_theirs, up_mine)], axis=0
    )
    up_other = to_other_core(up_own)
    up_all = jnp.concatenate([up_own, up_other], axis=1)
    out_other = to_other_core(out_weight)
    out_both = jnp.concatenate([out_weight, out_other], axis=0)

    def group_products(group):
        left = []
        for d in group:
            one, two = first_ring.blocks[d], second_ring.blocks[d]
            left.append(jnp.concatenate(
                [one[:, :part_units], two[:, :part_units], one[:, part_units:], two[:, part_units:]], axis=1
            ))
        product = times_transposed(jnp.concatenate(left, axis=0), up_all).astype(BF16)
        return product.reshape(pieces, len(group) * rows // pieces, 2 * feats)

    def piece_sums(product):
        return lax.all_to_all(product, ("y_hi", "y_lo", "x"), 0, 0, tiled=True)

    def input_piece(arrived, group):
        piece = len(group) * rows // pieces
        start = ((y_hi * 2 + y_lo) * N_X + x) * piece

        def rows_here(array):
            blocks = [lax.dynamic_slice_in_dim(array, block_start(d), rows, 0) for d in group]
            return lax.dynamic_slice_in_dim(jnp.concatenate(blocks, axis=0), start, piece, 0)

        mine, theirs = rows_here(cot), rows_here(cot_theirs)
        cot_part = jnp.concatenate(
            [jnp.where(y_hi == 0, mine, theirs), jnp.where(y_hi == 0, theirs, mine)], axis=1
        )
        return (jnp.sum(arrived.astype(F32), axis=0) + cot_part.astype(F32)).astype(BF16)

    def out_products(total):
        piece = total.shape[0]
        copies = jnp.stack([total[:, :feats], total[:, feats:]])[:, None]
        copies = jnp.broadcast_to(copies, (2, 2 * N_X, piece, feats))
        whole = lax.all_to_all(
            copies.reshape(pieces, piece, feats), ("y_hi", "y_lo", "x"), 0, 0, tiled=True
        )
        return times_transposed(whole.reshape(pieces * piece, feats), out_both).astype(BF16)

    first_arrived = first_ring.step()
    second_arrived = second_ring.step()
    first_second = first_ring.step()
    second_second = second_ring.step(*first_arrived, up_theirs)
    first_third = first_ring.step(*second_arrived)
    second_ring.step(*first_second)
    near_products = group_products(NEAR)
    near_sums = piece_sums(near_products)
    first_ring.step(*second_second)
    second_ring.step(*first_third, near_products)
    far_sums = piece_sums(after(group_products(FAR), near_sums))
    near_total = input_piece(near_sums, NEAR)
    far_total = input_piece(far_sums, FAR)

    far_product = out_products(far_total)
    near_product = out_products(after(near_total, far_product))

    def part(d):
        product, group = (near_product, NEAR) if d in NEAR else (far_product, FAR)
        at = group.index(d) * rows
        return product[at:at + rows]

    ring = Scatter(part, offset=1)
    for _ in range(4):
        ring.step()
    sums = ring.result().astype(BF16)
    width = sums.shape[1] // 2
    for_zero = jnp.where(core == 0, sums[:, :width], sums[:, width:])
    for_one = jnp.where(core == 0, sums[:, width:], sums[:, :width])
    here = to_swapped(jnp.where(y_hi == 0, for_zero, for_one))
    there = move(
        jnp.where(y_hi == 0, for_one, for_zero), lambda c, h, z, l, x: (1 - h, c, z, l, x)
    )
    return added(here, there).astype(BF16)


def solution(mesh):
    fine = Mesh(mesh.devices.reshape(2, 2, N_Z, 2, N_X), AXES)
    in_specs = (
        P(None, ROW),
        P(ROW, COLUMN),
        P(ROW, COLUMN),
        P(COLUMN, ROW),
        P(COLUMN, ROW),
    )
    return jax.shard_map(body, mesh=fine, in_specs=in_specs, out_specs=P(ROW, COLUMN), check_vma=False)
```

```python
import jax
import jax.numpy as jnp
from jax import lax
from jax.sharding import Mesh, PartitionSpec as P

N_Z = 8
N_X = 4
AXES = ("section", "y_hi", "z", "y_lo", "x")
ROW = ("y_hi", "z")
COLUMN = ("section", "y_lo", "x")
BF16 = jnp.bfloat16
F32 = jnp.float32
NEAR, FAR = (0, 1, -1, 2), (3, -3, -2, 4)


def gelu_slope(value):
    inner = 0.7978845608 * (value + 0.044715 * value * value * value)
    tanh_part = jnp.tanh(inner)
    derivative = 0.7978845608 * (1.0 + 3.0 * 0.044715 * value * value)
    return 0.5 * (1.0 + tanh_part) + 0.5 * value * (1.0 - tanh_part * tanh_part) * derivative


def times_transposed(left, right):
    return lax.dot_general(
        left, right, (((1,), (1,)), ((), ())), preferred_element_type=F32
    )


def move(value, where):
    pairs = []
    for core in range(2):
        for y_hi in range(2):
            for z in range(N_Z):
                for y_lo in range(2):
                    for x in range(N_X):
                        c, h, k, l, i = where(core, y_hi, z, y_lo, x)
                        source = ((core * 2 + y_hi) * N_Z + z) * 2 * N_X + y_lo * N_X + x
                        target = ((c * 2 + h) * N_Z + k % N_Z) * 2 * N_X + l * N_X + i % N_X
                        pairs.append((source, target))
    return lax.ppermute(value, AXES, pairs)


def to_other_core(value):
    return move(value, lambda c, h, z, l, x: (1 - c, h, z, l, x))


def to_y_hi(value):
    return move(value, lambda c, h, z, l, x: (c, 1 - h, z, l, x))


def to_swapped(value):
    return move(value, lambda c, h, z, l, x: (h, c, z, l, x))


def along_z(value, sign, own):
    def where(c, h, z, l, x):
        half = c if own else 1 - c
        return c, h, z + (sign if half == 0 else -sign), l, x
    return move(value, where)


def added(*terms):
    total = terms[0].astype(F32)
    for term in terms[1:]:
        total = total + term.astype(F32)
    return total


def after(value, *others):
    return lax.optimization_barrier((value, *others))[0]


class Scatter:
    def __init__(self, part, own=True):
        self.part, self.left, self.own = part, 4, own
        self.ahead = self.back = None

    def step(self, *waits):
        mine = self.part(self.left)
        behind = 1 - self.left
        far = self.part(behind) if -4 < behind < 0 else None
        if self.ahead is not None:
            mine = added(mine, self.ahead)
        if self.back is not None and far is not None:
            far = added(far, self.back)
        mine = mine.astype(BF16)
        far = None if far is None else far.astype(BF16)
        if far is not None:
            mine, far = lax.optimization_barrier((mine, far, *waits))[:2]
        elif waits:
            mine = after(mine, *waits)
        self.ahead = along_z(mine, 1, self.own)
        if far is not None:
            self.back = along_z(far, -1, self.own)
        self.left -= 1
        return self.arrived()

    def arrived(self):
        return [self.ahead, self.back]

    def result(self):
        return added(self.part(0), self.ahead, self.back)


class Gather:
    def __init__(self, block):
        self.blocks, self.distance = {0: block}, 0
        self.ahead = self.back = block

    def step(self, *waits):
        self.distance += 1
        ahead, back = lax.optimization_barrier((self.ahead, self.back, *waits))[:2]
        self.ahead = along_z(ahead, 1, True)
        self.blocks[4 if self.distance == 4 else -self.distance] = self.ahead
        if self.distance < 4:
            self.back = along_z(back, -1, True)
            self.blocks[self.distance] = self.back
        return [self.ahead, self.back]


def body(cotangent, pre_activation, up_weight, down_weight, out_weight):
    tokens, feats = cotangent.shape
    half_tokens = tokens // 2
    rows = half_tokens // N_Z
    pieces = 4 * N_X
    core = lax.axis_index("section")
    y_hi = lax.axis_index("y_hi")
    z = lax.axis_index("z")
    y_lo = lax.axis_index("y_lo")
    x = lax.axis_index("x")

    def block_start(distance, own=True):
        way = 1 - 2 * core if own else 2 * core - 1
        return ((z + way * distance + N_Z) % N_Z) * rows

    def half_of(array, index, axis):
        size = array.shape[axis] // 2
        return lax.dynamic_slice_in_dim(array, index * size, size, axis)

    def rows_here(array, group, above):
        piece = len(group) * rows // pieces
        blocks = [lax.dynamic_slice_in_dim(array, block_start(d), rows, 0) for d in group]
        start = ((above * 2 + y_lo) * N_X + x) * piece
        return lax.dynamic_slice_in_dim(jnp.concatenate(blocks, axis=0), start, piece, 0)

    cot = half_of(cotangent, core, 0)

    def ring_of(left, own):
        product = times_transposed(left, down_weight).astype(BF16)
        return Scatter(
            lambda d: lax.dynamic_slice_in_dim(product, block_start(d, own), rows, 0), own
        )

    own_ring = ring_of(cot, True)
    other_ring = ring_of(half_of(cotangent, 1 - core, 0), False)
    act_first = to_swapped(half_of(pre_activation, core, 1))
    act_second = move(
        half_of(pre_activation, 1 - core, 1), lambda c, h, z, l, x: (h, 1 - c, z, l, x)
    )
    up_mine = half_of(up_weight, y_hi, 1)
    up_theirs = to_y_hi(half_of(up_weight, 1 - y_hi, 1))
    own_first = own_ring.step()
    other_first = other_ring.step()
    own_second = own_ring.step()
    other_second = other_ring.step(*own_first)
    own_third = own_ring.step(*other_first)
    other_third = other_ring.step(*own_second)
    own_ring.step(*other_second)
    other_ring.step(*own_third, act_first, act_second)

    own_sums, other_sums = own_ring.result(), other_ring.result()
    own_arrived = to_y_hi(half_of(own_sums, 1 - y_hi, 1).astype(BF16))
    here_arrived = to_other_core(half_of(other_sums, y_hi, 1).astype(BF16))
    there_arrived = move(
        half_of(other_sums, 1 - y_hi, 1).astype(BF16), lambda c, h, z, l, x: (1 - c, 1 - h, z, l, x)
    )
    act_first, act_second = after(act_first, *other_third), after(act_second, *other_third)
    straight = core == y_hi
    slope_own = gelu_slope(jnp.where(straight, act_first, act_second).astype(F32))
    slope_other = gelu_slope(jnp.where(straight, act_second, act_first).astype(F32))
    first_grad = (added(half_of(own_sums, y_hi, 1), own_arrived) * slope_own).astype(BF16)
    first_ring = Gather(first_grad)
    slope_other = after(slope_other, first_grad)
    second_ring = Gather((added(here_arrived, there_arrived) * slope_other).astype(BF16))

    up_theirs = after(up_theirs, *other_third)
    up_own = jnp.concatenate(
        [jnp.where(y_hi == 0, up_mine, up_theirs), jnp.where(y_hi == 0, up_theirs, up_mine)], axis=0
    )
    up_other = to_other_core(up_own)
    up_all = jnp.concatenate([up_own, up_other], axis=1)
    late_cot, late_out = after(cot, first_grad), after(out_weight, first_grad)
    out_both = jnp.concatenate([out_weight, to_other_core(late_out)], axis=0)

    def rows_here(group, above):
        distance = lax.dynamic_index_in_dim(
            jnp.array(group, jnp.int32), above * 2 + y_lo, 0, keepdims=False
        )
        piece = len(group) * rows // pieces
        return lax.dynamic_slice_in_dim(late_cot, block_start(distance) + x * piece, piece, 0)

    cot_sent = [rows_here(group, 1 - y_hi) for group in (NEAR, FAR)]
    cot_arrived = to_y_hi(jnp.concatenate(cot_sent, axis=0))
    near_count = cot_sent[0].shape[0]

    def block_products(group):
        left = [jnp.concatenate([first_ring.blocks[d], second_ring.blocks[d]], axis=1) for d in group]
        return times_transposed(jnp.concatenate(left, axis=0), up_all).astype(BF16)

    def in_pieces(product):
        return product.reshape(pieces, product.shape[0] // pieces, 2 * feats)

    def piece_sums(product):
        return lax.all_to_all(product, ("y_hi", "y_lo", "x"), 0, 0, tiled=True)

    def input_piece(arrived, group, theirs):
        mine = rows_here(group, y_hi)
        cot_part = jnp.concatenate(
            [jnp.where(y_hi == 0, mine, theirs), jnp.where(y_hi == 0, theirs, mine)], axis=1
        )
        return (jnp.sum(arrived.astype(F32), axis=0) + cot_part.astype(F32)).astype(BF16)

    def out_products(total):
        piece = total.shape[0]
        copies = jnp.stack([total[:, :feats], total[:, feats:]])[:, None]
        copies = jnp.broadcast_to(copies, (2, 2 * N_X, piece, feats))
        whole = lax.all_to_all(
            copies.reshape(pieces, piece, feats), ("y_hi", "y_lo", "x"), 0, 0, tiled=True
        )
        return times_transposed(whole.reshape(pieces * piece, feats), out_both).astype(BF16)

    first_arrived = first_ring.step()
    second_arrived = second_ring.step()
    first_second = first_ring.step()
    second_second = second_ring.step(*first_arrived, up_other)
    first_third = first_ring.step(*second_arrived)
    second_ring.step(*first_second)
    near_products = in_pieces(block_products(NEAR))
    near_sums = piece_sums(near_products)
    first_ring.step(*second_second)
    second_ring.step(*first_third, near_products)
    far_products = jnp.concatenate([block_products(FAR[:3]), block_products(FAR[3:])], axis=0)
    far_sums = piece_sums(after(in_pieces(far_products), near_sums))
    near_total = input_piece(near_sums, NEAR, cot_arrived[:near_count])
    far_total = input_piece(far_sums, FAR, cot_arrived[near_count:])

    far_product = out_products(far_total)
    near_product = out_products(after(near_total, far_product))

    def part(d):
        product, group = (near_product, NEAR) if d in NEAR else (far_product, FAR)
        at = group.index(d) * rows
        return product[at:at + rows]

    ring = Scatter(part)
    for _ in range(4):
        ring.step()
    sums = ring.result().astype(BF16)
    width = sums.shape[1] // 2
    for_zero = jnp.where(core == 0, sums[:, :width], sums[:, width:])
    for_one = jnp.where(core == 0, sums[:, width:], sums[:, :width])
    here = to_swapped(jnp.where(y_hi == 0, for_zero, for_one))
    there = move(
        jnp.where(y_hi == 0, for_one, for_zero), lambda c, h, z, l, x: (1 - h, c, z, l, x)
    )
    return added(here, there).astype(BF16)


def solution(mesh):
    fine = Mesh(mesh.devices.reshape(2, 2, N_Z, 2, N_X), AXES)
    in_specs = (
        P(None, ROW),
        P(ROW, COLUMN),
        P(ROW, COLUMN),
        P(COLUMN, ROW),
        P(COLUMN, ROW),
    )
    return jax.shard_map(body, mesh=fine, in_specs=in_specs, out_specs=P(ROW, COLUMN), check_vma=False)
```

```python
import jax
import jax.numpy as jnp
from jax import lax
from jax.sharding import Mesh, PartitionSpec as P

N_Z = 8
N_X = 4
AXES = ("section", "y_hi", "z", "y_lo", "x")
ROW = ("y_hi", "z")
COLUMN = ("section", "y_lo", "x")
BF16 = jnp.bfloat16
F32 = jnp.float32
NEAR, FAR = (0, 1, -1, 2), (3, -3, -2, 4)


def gelu_slope(value):
    inner = 0.7978845608 * (value + 0.044715 * value * value * value)
    tanh_part = jnp.tanh(inner)
    derivative = 0.7978845608 * (1.0 + 3.0 * 0.044715 * value * value)
    return 0.5 * (1.0 + tanh_part) + 0.5 * value * (1.0 - tanh_part * tanh_part) * derivative


def times_transposed(left, right):
    return lax.dot_general(
        left, right, (((1,), (1,)), ((), ())), preferred_element_type=F32
    )


def move(value, where):
    pairs = []
    for core in range(2):
        for y_hi in range(2):
            for z in range(N_Z):
                for y_lo in range(2):
                    for x in range(N_X):
                        c, h, k, l, i = where(core, y_hi, z, y_lo, x)
                        source = ((core * 2 + y_hi) * N_Z + z) * 2 * N_X + y_lo * N_X + x
                        target = ((c * 2 + h) * N_Z + k % N_Z) * 2 * N_X + l * N_X + i % N_X
                        pairs.append((source, target))
    return lax.ppermute(value, AXES, pairs)


def to_y_hi(value):
    return move(value, lambda c, h, z, l, x: (c, 1 - h, z, l, x))


def along_z(value, sign):
    return move(value, lambda c, h, z, l, x: (c, h, z + sign, l, x))


def added(*terms):
    total = terms[0].astype(F32)
    for term in terms[1:]:
        total = total + term.astype(F32)
    return total


def after(value, *others):
    return lax.optimization_barrier((value, *others))[0]


class Scatter:
    def __init__(self, part, way):
        self.part, self.left, self.way = part, 4, way
        self.ahead = self.back = None

    def step(self, *waits):
        mine = self.part(self.way * self.left)
        far = self.part(self.way * (1 - self.left)) if self.left > 1 else None
        if self.ahead is not None:
            mine = added(mine, self.ahead)
            far = None if far is None else added(far, self.back)
        mine = mine.astype(BF16)
        if far is not None:
            mine, far = lax.optimization_barrier((mine, far.astype(BF16), *waits))[:2]
        elif waits:
            mine = after(mine, *waits)
        self.ahead = along_z(mine, self.way)
        if far is not None:
            self.back = along_z(far, -self.way)
        self.left -= 1
        return [self.ahead, self.back]

    def result(self):
        return added(self.part(0), self.ahead, self.back)


class Gather:
    def __init__(self, block, way):
        self.blocks, self.distance, self.way = {0: block}, 0, way
        self.ahead = self.back = block

    def step(self, *waits):
        self.distance += 1
        ahead, back = lax.optimization_barrier((self.ahead, self.back, *waits))[:2]
        self.ahead = along_z(ahead, self.way)
        self.blocks[4 if self.distance == 4 else -self.way * self.distance] = self.ahead
        if self.distance < 4:
            self.back = along_z(back, -self.way)
            self.blocks[self.way * self.distance] = self.back
        return [self.ahead, self.back]


def body(cotangent, pre_activation, up_weight, down_weight, out_weight):
    tokens, feats = cotangent.shape
    half_tokens = tokens // 2
    rows = half_tokens // N_Z
    pieces = 4 * N_X
    piece = 4 * rows // pieces
    core = lax.axis_index("section")
    y_hi = lax.axis_index("y_hi")
    z = lax.axis_index("z")
    y_lo = lax.axis_index("y_lo")
    x = lax.axis_index("x")

    def start_of(half, e):
        return half * half_tokens + ((z + e + N_Z) % N_Z) * rows

    def block_of(array, e):
        return lax.dynamic_slice_in_dim(array, start_of(0, e), rows, 1)

    up_theirs = to_y_hi(up_weight)

    width = down_weight.shape[0] // 2
    halves = cotangent.reshape(2, half_tokens, feats)

    def ring_of(weight, way):
        ends = (4 * way, -3 * way)
        first = jnp.concatenate([block_of(halves, e) for e in ends], axis=0)
        first = times_transposed(first.reshape(4 * rows, feats), weight).astype(BF16)
        first = first.reshape(2, 2, rows, width)
        rest = after(cotangent, first)
        rest = times_transposed(rest, weight).astype(BF16).reshape(2, half_tokens, width)

        def part(e):
            return first[ends.index(e)] if e in ends else block_of(rest, e)

        return Scatter(part, way)

    first_sums = ring_of(down_weight[:width], 1)
    second_sums = ring_of(down_weight[width:], -1)
    first_one = first_sums.step()
    second_one = second_sums.step()
    first_two = first_sums.step()
    second_two = second_sums.step(*first_one)
    first_three = first_sums.step(*second_one)
    second_three = second_sums.step(*first_two)
    first_sums.step(*second_two, up_theirs)
    second_sums.step(*first_three)

    slope = gelu_slope(after(pre_activation, *second_three).astype(F32))

    def grad_of(sums, slope):
        total = sums.result()
        mine = lax.dynamic_index_in_dim(total, y_hi, 0, keepdims=False)
        theirs = lax.dynamic_index_in_dim(total, 1 - y_hi, 0, keepdims=False)
        return (added(mine, to_y_hi(theirs.astype(BF16))) * slope).astype(BF16)

    first_grad = grad_of(first_sums, slope[:, :width])
    first_ring = Gather(first_grad, 1)
    second_ring = Gather(grad_of(second_sums, after(slope[:, width:], first_grad)), -1)

    up_all = jnp.concatenate([up_weight, after(up_theirs, *second_three)], axis=0)
    late_cot, late_out = after(cotangent, first_grad), after(out_weight, first_grad)
    out_all = jnp.concatenate([out_weight, to_y_hi(late_out)], axis=1)

    def rows_here(half, group):
        distance = lax.dynamic_index_in_dim(
            jnp.array(group, jnp.int32), core * 2 + y_lo, 0, keepdims=False
        )
        return lax.dynamic_slice_in_dim(late_cot, start_of(half, distance) + x * piece, piece, 0)

    cot_arrived = to_y_hi(
        jnp.concatenate([rows_here(1 - y_hi, group) for group in (NEAR, FAR)], axis=0)
    )

    def block_products(group):
        left = [jnp.concatenate([first_ring.blocks[e], second_ring.blocks[e]], axis=1) for e in group]
        return times_transposed(jnp.concatenate(left, axis=0), up_all).astype(BF16)

    def group_products(group):
        product = jnp.concatenate([block_products(group[:3]), block_products(group[3:])], axis=0)
        return product.reshape(pieces, piece, 2 * feats)

    def piece_sums(product):
        return lax.all_to_all(product, COLUMN, 0, 0, tiled=True)

    def input_piece(arrived, group, theirs):
        cot_part = jnp.concatenate([rows_here(y_hi, group), theirs], axis=1)
        return (jnp.sum(arrived.astype(F32), axis=0) + cot_part.astype(F32)).astype(BF16)

    def out_products(total):
        copies = jnp.broadcast_to(total[None], (pieces, piece, 2 * feats))
        whole = lax.all_to_all(copies, COLUMN, 0, 0, tiled=True)
        return times_transposed(whole.reshape(4 * rows, 2 * feats), out_all).astype(BF16)

    first_arrived = first_ring.step()
    second_arrived = second_ring.step()
    first_second = first_ring.step()
    second_second = second_ring.step(*first_arrived)
    first_third = first_ring.step(*second_arrived)
    second_ring.step(*first_second, cot_arrived)
    near_products = group_products(NEAR)
    near_sums = piece_sums(near_products)
    first_ring.step(*second_second)
    second_ring.step(*first_third, near_products)
    far_sums = piece_sums(after(group_products(FAR), near_sums))
    near_total = input_piece(near_sums, NEAR, cot_arrived[:piece])
    far_total = input_piece(far_sums, FAR, cot_arrived[piece:])

    far_product = out_products(far_total)
    near_product = out_products(after(near_total, far_product))

    def part(e):
        e = 4 if e == -4 else e
        product, group = (near_product, NEAR) if e in NEAR else (far_product, FAR)
        at = group.index(e) * rows
        return product[at:at + rows]

    ring = Scatter(part, 1)
    for _ in range(4):
        ring.step()
    return ring.result().astype(BF16)


def solution(mesh):
    fine = Mesh(mesh.devices.reshape(2, 2, N_Z, 2, N_X), AXES)
    in_specs = (
        P(None, ROW),
        P(ROW, COLUMN),
        P(ROW, COLUMN),
        P(COLUMN, ROW),
        P(COLUMN, ROW),
    )
    return jax.shard_map(body, mesh=fine, in_specs=in_specs, out_specs=P(ROW, COLUMN), check_vma=False)
```

```python
import jax
import jax.numpy as jnp
from jax import lax
from jax.sharding import Mesh, PartitionSpec as P

N_Z = 8
N_X = 4
AXES = ("section", "y_hi", "z", "y_lo", "x")
ROW = ("y_hi", "z")
COLUMN = ("section", "y_lo", "x")
BF16 = jnp.bfloat16
F32 = jnp.float32
ORDER = (0, 1, -1, 2, -2, 3, -3, 4)
GROUPS = (ORDER[:3], ORDER[3:5], ORDER[5:])


def gelu_slope(value):
    inner = 0.7978845608 * (value + 0.044715 * value * value * value)
    tanh_part = jnp.tanh(inner)
    derivative = 0.7978845608 * (1.0 + 3.0 * 0.044715 * value * value)
    return 0.5 * (1.0 + tanh_part) + 0.5 * value * (1.0 - tanh_part * tanh_part) * derivative


def times_transposed(left, right):
    return lax.dot_general(
        left, right, (((1,), (1,)), ((), ())), preferred_element_type=F32
    )


def move(value, where):
    pairs = []
    for core in range(2):
        for y_hi in range(2):
            for z in range(N_Z):
                for y_lo in range(2):
                    for x in range(N_X):
                        c, h, k, l, i = where(core, y_hi, z, y_lo, x)
                        source = ((core * 2 + y_hi) * N_Z + z) * 2 * N_X + y_lo * N_X + x
                        target = ((c * 2 + h) * N_Z + k % N_Z) * 2 * N_X + l * N_X + i % N_X
                        pairs.append((source, target))
    return lax.ppermute(value, AXES, pairs)


def to_y_hi(value):
    return move(value, lambda c, h, z, l, x: (c, 1 - h, z, l, x))


def to_other_core(value):
    return move(value, lambda c, h, z, l, x: (1 - c, h, z, l, x))


def along_z(value, sign):
    return move(value, lambda c, h, z, l, x: (c, h, z + sign, l, x))


def added(*terms):
    total = terms[0].astype(F32)
    for term in terms[1:]:
        total = total + term.astype(F32)
    return total


def after(value, *others):
    return lax.optimization_barrier((value, *others))[0]


class Scatter:
    def __init__(self, part, way):
        self.part, self.left, self.way = part, 4, way
        self.ahead = self.back = None

    def step(self, *waits):
        mine = self.part(self.way * self.left)
        far = self.part(self.way * (1 - self.left)) if self.left > 1 else None
        if self.ahead is not None:
            mine = added(mine, self.ahead)
            far = None if far is None else added(far, self.back)
        mine = mine.astype(BF16)
        if far is not None:
            mine, far = lax.optimization_barrier((mine, far.astype(BF16), *waits))[:2]
        elif waits:
            mine = after(mine, *waits)
        self.ahead = along_z(mine, self.way)
        if far is not None:
            self.back = along_z(far, -self.way)
        self.left -= 1
        return [self.ahead, self.back]

    def result(self):
        return added(self.part(0), self.ahead, self.back)


class Gather:
    def __init__(self, block, way):
        self.blocks, self.distance, self.way = {0: block}, 0, way
        self.ahead = self.back = block

    def step(self, *waits):
        self.distance += 1
        ahead, back = lax.optimization_barrier((self.ahead, self.back, *waits))[:2]
        self.ahead = along_z(ahead, self.way)
        self.blocks[4 if self.distance == 4 else -self.way * self.distance] = self.ahead
        if self.distance < 4:
            self.back = along_z(back, -self.way)
            self.blocks[self.way * self.distance] = self.back
        return [self.ahead, self.back]


def body(cotangent, pre_activation, up_weight, down_weight, out_weight):
    tokens, feats = cotangent.shape
    half_tokens = tokens // 2
    rows = half_tokens // N_Z
    pieces = 4 * N_X
    piece = rows // pieces
    core = lax.axis_index("section")
    y_hi = lax.axis_index("y_hi")
    z = lax.axis_index("z")
    y_lo = lax.axis_index("y_lo")
    x = lax.axis_index("x")

    def start_of(half, e):
        return half * half_tokens + ((z + e + N_Z) % N_Z) * rows

    def block_of(array, e):
        return lax.dynamic_slice_in_dim(array, start_of(0, e), rows, 1)

    up_half = feats // 2
    up_theirs = to_y_hi(up_weight[:up_half])

    width = down_weight.shape[0] // 2
    halves = cotangent.reshape(2, half_tokens, feats)

    def ring_of(weight, way):
        ends = (4 * way, -3 * way)
        first = jnp.concatenate([block_of(halves, e) for e in ends], axis=0)
        first = times_transposed(first.reshape(4 * rows, feats), weight).astype(BF16)
        first = first.reshape(2, 2, rows, width)
        rest = after(cotangent, first)
        rest = times_transposed(rest, weight).astype(BF16).reshape(2, half_tokens, width)

        def part(e):
            return first[ends.index(e)] if e in ends else block_of(rest, e)

        return Scatter(part, way)

    first_sums = ring_of(down_weight[:width], 1)
    second_sums = ring_of(down_weight[width:], -1)
    first_one = first_sums.step()
    second_one = second_sums.step()
    first_two = first_sums.step()
    second_two = second_sums.step(*first_one)
    first_three = first_sums.step(*second_one)
    second_three = second_sums.step(*first_two)
    up_more = to_y_hi(after(up_weight[up_half:], *first_two))
    first_sums.step(*second_two, up_theirs)
    second_sums.step(*first_three)

    slope = gelu_slope(after(pre_activation, *second_three).astype(F32))

    def grad_of(sums, slope):
        total = sums.result()
        mine = lax.dynamic_index_in_dim(total, y_hi, 0, keepdims=False)
        theirs = lax.dynamic_index_in_dim(total, 1 - y_hi, 0, keepdims=False)
        return (added(mine, to_y_hi(theirs.astype(BF16))) * slope).astype(BF16)

    first_grad = grad_of(first_sums, slope[:, :width])
    first_ring = Gather(first_grad, 1)
    second_ring = Gather(grad_of(second_sums, after(slope[:, width:], first_grad)), -1)

    up_theirs, up_more = after(up_theirs, *second_three), after(up_more, *second_three)
    up_all = jnp.concatenate([up_weight, up_theirs, up_more], axis=0)
    late_cot, late_out = after(cotangent, first_grad), after(out_weight, first_grad)
    out_all = jnp.concatenate([out_weight, to_y_hi(late_out)], axis=1)

    place = (core * 2 + y_lo) * N_X + x

    def rows_here(half):
        blocks = late_cot.reshape(2, N_Z, pieces, piece, feats)
        blocks = lax.dynamic_slice(
            blocks, (half, 0, place, 0, 0), (1, N_Z, 1, piece, feats)
        ).reshape(N_Z, piece, feats)
        blocks = lax.dynamic_slice_in_dim(jnp.concatenate([blocks, blocks], axis=0), z, N_Z, 0)
        return jnp.concatenate([blocks[e % N_Z] for e in ORDER], axis=0)

    cot_arrived = to_y_hi(rows_here(1 - y_hi))

    def block_products(group):
        left = [jnp.concatenate([first_ring.blocks[e], second_ring.blocks[e]], axis=1) for e in group]
        return times_transposed(jnp.concatenate(left, axis=0), up_all).astype(BF16)

    def in_pieces(product):
        count = product.shape[0] // rows
        product = product.reshape(count, pieces, piece, 2 * feats).transpose(1, 0, 2, 3)
        return product.reshape(pieces, count * piece, 2 * feats)

    def piece_sums(product):
        return lax.all_to_all(product, COLUMN, 0, 0, tiled=True)

    first_arrived = first_ring.step()
    second_arrived = second_ring.step()
    first_second = first_ring.step()
    second_second = second_ring.step(*first_arrived)
    products = in_pieces(block_products(GROUPS[0]))
    sums = [piece_sums(products)]
    first_third = first_ring.step(*second_arrived)
    second_ring.step(*first_second, cot_arrived, products)
    products = in_pieces(block_products(GROUPS[1]))
    sums.append(piece_sums(after(products, sums[0])))
    first_ring.step(*second_second, sums[0])
    second_ring.step(*first_third, products)
    products = [block_products(GROUPS[2][:2]), block_products(GROUPS[2][2:])]
    sums.append(piece_sums(after(in_pieces(jnp.concatenate(products, axis=0)), sums[1])))
    cot_here = jnp.concatenate([after(rows_here(y_hi), *second_arrived), cot_arrived], axis=1)
    totals, at = [], 0
    for arrived in sums:
        count = arrived.shape[1]
        part_sum = jnp.sum(arrived.astype(F32), axis=0) + cot_here[at:at + count].astype(F32)
        totals.append(part_sum.astype(BF16))
        at += count

    total = jnp.concatenate(totals, axis=0)
    copies = jnp.broadcast_to(total[None], (2 * N_X, *total.shape))
    own_pieces = lax.all_to_all(copies, ("y_lo", "x"), 0, 0, tiled=True)
    other_pieces = to_other_core(own_pieces)

    def out_products(whole):
        product = times_transposed(whole.reshape(half_tokens // 2, 2 * feats), out_all)
        return product.astype(BF16).reshape(2 * N_X, N_Z, piece, -1)

    own_product, other_product = out_products(own_pieces), out_products(other_pieces)

    def part(e):
        at = ORDER.index(4 if e == -4 else e)
        both = jnp.concatenate([own_product[:, at], other_product[:, at]], axis=0)
        return both.reshape(rows, -1)

    ring = Scatter(part, 1)
    for _ in range(4):
        ring.step()
    result = ring.result().astype(BF16)
    swapped = jnp.concatenate([result[rows // 2:], result[:rows // 2]], axis=0)
    return jnp.where(core == 0, result, swapped)


def solution(mesh):
    fine = Mesh(mesh.devices.reshape(2, 2, N_Z, 2, N_X), AXES)
    in_specs = (
        P(None, ROW),
        P(ROW, COLUMN),
        P(ROW, COLUMN),
        P(COLUMN, ROW),
        P(COLUMN, ROW),
    )
    return jax.shard_map(body, mesh=fine, in_specs=in_specs, out_specs=P(ROW, COLUMN), check_vma=False)
```

```python
import jax
import jax.numpy as jnp
from jax import lax
from jax.sharding import Mesh, PartitionSpec as P

N_Z = 8
N_X = 4
AXES = ("section", "y_hi", "z", "y_lo", "x")
ROW = ("y_hi", "z")
COLUMN = ("section", "y_lo", "x")
BF16 = jnp.bfloat16
F32 = jnp.float32
ORDER = (0, 1, -1, 2, -2, 3, -3, 4)
GROUPS = (ORDER[:3], ORDER[3:])


def gelu_slope(value):
    inner = 0.7978845608 * (value + 0.044715 * value * value * value)
    tanh_part = jnp.tanh(inner)
    derivative = 0.7978845608 * (1.0 + 3.0 * 0.044715 * value * value)
    return 0.5 * (1.0 + tanh_part) + 0.5 * value * (1.0 - tanh_part * tanh_part) * derivative


def times_transposed(left, right):
    return lax.dot_general(
        left, right, (((1,), (1,)), ((), ())), preferred_element_type=F32
    )


def move(value, where):
    pairs = []
    for core in range(2):
        for y_hi in range(2):
            for z in range(N_Z):
                for y_lo in range(2):
                    for x in range(N_X):
                        c, h, k, l, i = where(core, y_hi, z, y_lo, x)
                        source = ((core * 2 + y_hi) * N_Z + z) * 2 * N_X + y_lo * N_X + x
                        target = ((c * 2 + h) * N_Z + k % N_Z) * 2 * N_X + l * N_X + i % N_X
                        pairs.append((source, target))
    return lax.ppermute(value, AXES, pairs)


def to_y_hi(value):
    return move(value, lambda c, h, z, l, x: (c, 1 - h, z, l, x))


def to_other_core(value):
    return move(value, lambda c, h, z, l, x: (1 - c, h, z, l, x))


def along_z(value, sign):
    return move(value, lambda c, h, z, l, x: (c, h, z + sign, l, x))


def added(*terms):
    total = terms[0].astype(F32)
    for term in terms[1:]:
        total = total + term.astype(F32)
    return total


def after(value, *others):
    return lax.optimization_barrier((value, *others))[0]


class Scatter:
    def __init__(self, part, way):
        self.part, self.left, self.way = part, 4, way
        self.ahead = self.back = None

    def step(self, *waits):
        mine = self.part(self.way * self.left)
        far = self.part(self.way * (1 - self.left)) if self.left > 1 else None
        if self.ahead is not None:
            mine = added(mine, self.ahead)
            far = None if far is None else added(far, self.back)
        mine = mine.astype(BF16)
        if far is not None:
            mine, far = lax.optimization_barrier((mine, far.astype(BF16), *waits))[:2]
        elif waits:
            mine = after(mine, *waits)
        self.ahead = along_z(mine, self.way)
        if far is not None:
            self.back = along_z(far, -self.way)
        self.left -= 1
        return [self.ahead, self.back]

    def result(self):
        return added(self.part(0), self.ahead, self.back)


class Gather:
    def __init__(self, block, way):
        self.blocks, self.distance, self.way = {0: block}, 0, way
        self.ahead = self.back = block

    def step(self, *waits):
        self.distance += 1
        ahead, back = lax.optimization_barrier((self.ahead, self.back, *waits))[:2]
        self.ahead = along_z(ahead, self.way)
        self.blocks[4 if self.distance == 4 else -self.way * self.distance] = self.ahead
        if self.distance < 4:
            self.back = along_z(back, -self.way)
            self.blocks[self.way * self.distance] = self.back
        return [self.ahead, self.back]


def body(cotangent, pre_activation, up_weight, down_weight, out_weight):
    tokens, feats = cotangent.shape
    half_tokens = tokens // 2
    rows = half_tokens // N_Z
    pieces = 4 * N_X
    piece = rows // pieces
    core = lax.axis_index("section")
    y_hi = lax.axis_index("y_hi")
    z = lax.axis_index("z")
    y_lo = lax.axis_index("y_lo")
    x = lax.axis_index("x")

    def start_of(half, e):
        return half * half_tokens + ((z + e + N_Z) % N_Z) * rows

    def block_of(array, e):
        return lax.dynamic_slice_in_dim(array, start_of(0, e), rows, 1)

    up_half = feats // 2
    up_theirs = to_y_hi(up_weight[:up_half])

    width = down_weight.shape[0] // 2
    halves = cotangent.reshape(2, half_tokens, feats)

    def ring_of(weight, way):
        ends = (4 * way, -3 * way)
        first = jnp.concatenate([block_of(halves, e) for e in ends], axis=0)
        first = times_transposed(first.reshape(4 * rows, feats), weight).astype(BF16)
        first = first.reshape(2, 2, rows, width)
        rest = after(cotangent, first)
        rest = times_transposed(rest, weight).astype(BF16).reshape(2, half_tokens, width)

        def part(e):
            return first[ends.index(e)] if e in ends else block_of(rest, e)

        return Scatter(part, way)

    first_sums = ring_of(down_weight[:width], 1)
    second_sums = ring_of(down_weight[width:], -1)
    first_one = first_sums.step()
    second_one = second_sums.step()
    first_two = first_sums.step()
    second_two = second_sums.step(*first_one)
    up_more = to_y_hi(after(up_weight[up_half:], *first_one))
    first_three = first_sums.step(*second_one, up_theirs)
    second_three = second_sums.step(*first_two)
    out_theirs = to_y_hi(after(out_weight, *first_two))
    first_sums.step(*second_two, up_more)
    second_sums.step(*first_three, out_theirs)

    slope = gelu_slope(after(pre_activation, *second_three).astype(F32))

    def grad_of(sums, slope):
        total = sums.result()
        mine = lax.dynamic_index_in_dim(total, y_hi, 0, keepdims=False)
        theirs = lax.dynamic_index_in_dim(total, 1 - y_hi, 0, keepdims=False)
        return (added(mine, to_y_hi(theirs.astype(BF16))) * slope).astype(BF16)

    first_grad = grad_of(first_sums, slope[:, :width])
    first_ring = Gather(first_grad, 1)
    second_ring = Gather(grad_of(second_sums, after(slope[:, width:], first_grad)), -1)

    up_theirs, up_more = after(up_theirs, *second_three), after(up_more, *second_three)
    up_all = jnp.concatenate([up_weight, up_theirs, up_more], axis=0)
    late_cot = after(cotangent, first_grad)
    out_all = jnp.concatenate([out_weight, out_theirs], axis=1)

    place = (core * 2 + y_lo) * N_X + x

    def rows_here(half):
        blocks = late_cot.reshape(2, N_Z, pieces, piece, feats)
        blocks = lax.dynamic_slice(
            blocks, (half, 0, place, 0, 0), (1, N_Z, 1, piece, feats)
        ).reshape(N_Z, piece, feats)
        blocks = lax.dynamic_slice_in_dim(jnp.concatenate([blocks, blocks], axis=0), z, N_Z, 0)
        return jnp.concatenate([blocks[e % N_Z] for e in ORDER], axis=0)

    cot_arrived = to_y_hi(rows_here(1 - y_hi))

    def block_products(group):
        left = [jnp.concatenate([first_ring.blocks[e], second_ring.blocks[e]], axis=1) for e in group]
        return times_transposed(jnp.concatenate(left, axis=0), up_all).astype(BF16)

    def in_pieces(product):
        count = product.shape[0] // rows
        product = product.reshape(count, pieces, piece, 2 * feats).transpose(1, 0, 2, 3)
        return product.reshape(pieces, count * piece, 2 * feats)

    def piece_sums(product):
        return lax.all_to_all(product, COLUMN, 0, 0, tiled=True)

    first_arrived = first_ring.step()
    second_arrived = second_ring.step()
    first_second = first_ring.step()
    second_second = second_ring.step(*first_arrived)
    products = in_pieces(block_products(GROUPS[0]))
    sums = [piece_sums(products)]
    first_third = first_ring.step(*second_arrived)
    second_ring.step(*first_second, cot_arrived, products)
    first_ring.step(*second_second)
    second_ring.step(*first_third)
    products = [block_products(GROUPS[1][:4]), block_products(GROUPS[1][4:])]
    sums.append(piece_sums(after(in_pieces(jnp.concatenate(products, axis=0)), sums[0])))
    cot_here = jnp.concatenate([after(rows_here(y_hi), *second_arrived), cot_arrived], axis=1)
    totals, at = [], 0
    for arrived in sums:
        count = arrived.shape[1]
        part_sum = jnp.sum(arrived.astype(F32), axis=0) + cot_here[at:at + count].astype(F32)
        totals.append(part_sum.astype(BF16))
        at += count

    total = jnp.concatenate(totals, axis=0)
    copies = jnp.broadcast_to(total[None], (2 * N_X, *total.shape))
    own_pieces = lax.all_to_all(copies, ("y_lo", "x"), 0, 0, tiled=True)
    other_pieces = to_other_core(own_pieces)

    def out_products(whole):
        product = times_transposed(whole.reshape(half_tokens // 2, 2 * feats), out_all)
        return product.astype(BF16).reshape(2 * N_X, N_Z, piece, -1)

    own_product, other_product = out_products(own_pieces), out_products(other_pieces)

    def part(e):
        at = ORDER.index(4 if e == -4 else e)
        both = jnp.concatenate([own_product[:, at], other_product[:, at]], axis=0)
        return both.reshape(rows, -1)

    ring = Scatter(part, 1)
    for _ in range(4):
        ring.step()
    result = ring.result().astype(BF16)
    swapped = jnp.concatenate([result[rows // 2:], result[:rows // 2]], axis=0)
    return jnp.where(core == 0, result, swapped)


def solution(mesh):
    fine = Mesh(mesh.devices.reshape(2, 2, N_Z, 2, N_X), AXES)
    in_specs = (
        P(None, ROW),
        P(ROW, COLUMN),
        P(ROW, COLUMN),
        P(COLUMN, ROW),
        P(COLUMN, ROW),
    )
    return jax.shard_map(body, mesh=fine, in_specs=in_specs, out_specs=P(ROW, COLUMN), check_vma=False)
```

```python
import jax
import jax.numpy as jnp
from jax import lax
from jax.sharding import Mesh, PartitionSpec as P

N_Z = 8
N_X = 4
AXES = ("section", "y_hi", "z", "y_lo", "x")
ROW = ("y_hi", "z")
COLUMN = ("section", "y_lo", "x")
BF16 = jnp.bfloat16
F32 = jnp.float32
ORDER = (0, 1, -1, 2, -2, 3, -3, 4)
GROUPS = (ORDER[:3], ORDER[3:])


def gelu_slope(value):
    inner = 0.7978845608 * (value + 0.044715 * value * value * value)
    tanh_part = jnp.tanh(inner)
    derivative = 0.7978845608 * (1.0 + 3.0 * 0.044715 * value * value)
    return 0.5 * (1.0 + tanh_part) + 0.5 * value * (1.0 - tanh_part * tanh_part) * derivative


def times_transposed(left, right):
    return lax.dot_general(
        left, right, (((1,), (1,)), ((), ())), preferred_element_type=F32
    )


def move(value, where):
    pairs = []
    for core in range(2):
        for y_hi in range(2):
            for z in range(N_Z):
                for y_lo in range(2):
                    for x in range(N_X):
                        c, h, k, l, i = where(core, y_hi, z, y_lo, x)
                        source = ((core * 2 + y_hi) * N_Z + z) * 2 * N_X + y_lo * N_X + x
                        target = ((c * 2 + h) * N_Z + k % N_Z) * 2 * N_X + l * N_X + i % N_X
                        pairs.append((source, target))
    return lax.ppermute(value, AXES, pairs)


def to_y_hi(value):
    return move(value, lambda c, h, z, l, x: (c, 1 - h, z, l, x))


def to_other_core(value):
    return move(value, lambda c, h, z, l, x: (1 - c, h, z, l, x))


def along_z(value, sign):
    return move(value, lambda c, h, z, l, x: (c, h, z + sign, l, x))


def added(*terms):
    total = terms[0].astype(F32)
    for term in terms[1:]:
        total = total + term.astype(F32)
    return total


def after(value, *others):
    return lax.optimization_barrier((value, *others))[0]


class Scatter:
    def __init__(self, part, way):
        self.part, self.left, self.way = part, 4, way
        self.ahead = self.back = None

    def step(self, *waits):
        mine = self.part(self.way * self.left)
        far = self.part(self.way * (1 - self.left)) if self.left > 1 else None
        if self.ahead is not None:
            mine = added(mine, self.ahead)
            far = None if far is None else added(far, self.back)
        mine = mine.astype(BF16)
        if far is not None:
            mine, far = lax.optimization_barrier((mine, far.astype(BF16), *waits))[:2]
        elif waits:
            mine = after(mine, *waits)
        self.ahead = along_z(mine, self.way)
        if far is not None:
            self.back = along_z(far, -self.way)
        self.left -= 1
        return [self.ahead, self.back]

    def result(self):
        return added(self.part(0), self.ahead, self.back)


class Gather:
    def __init__(self, block, way):
        self.blocks, self.distance, self.way = {0: block}, 0, way
        self.ahead = self.back = block

    def step(self, *waits):
        self.distance += 1
        ahead, back = lax.optimization_barrier((self.ahead, self.back, *waits))[:2]
        self.ahead = along_z(ahead, self.way)
        self.blocks[4 if self.distance == 4 else -self.way * self.distance] = self.ahead
        if self.distance < 4:
            self.back = along_z(back, -self.way)
            self.blocks[self.way * self.distance] = self.back
        return [self.ahead, self.back]


def body(cotangent, pre_activation, up_weight, down_weight, out_weight):
    tokens, feats = cotangent.shape
    half_tokens = tokens // 2
    rows = half_tokens // N_Z
    pieces = 4 * N_X
    piece = rows // pieces
    core = lax.axis_index("section")
    y_hi = lax.axis_index("y_hi")
    z = lax.axis_index("z")
    y_lo = lax.axis_index("y_lo")
    x = lax.axis_index("x")

    def start_of(half, e):
        return half * half_tokens + ((z + e + N_Z) % N_Z) * rows

    def block_of(array, e):
        return lax.dynamic_slice_in_dim(array, start_of(0, e), rows, 1)

    up_half = feats // 2

    width = down_weight.shape[0] // 2
    halves = cotangent.reshape(2, half_tokens, feats)

    def ring_of(weight, way):
        ends = (4 * way, -3 * way)
        first = jnp.concatenate([block_of(halves, e) for e in ends], axis=0)
        first = times_transposed(first.reshape(4 * rows, feats), weight).astype(BF16)
        first = first.reshape(2, 2, rows, width)
        rest = after(cotangent, first)
        rest = times_transposed(rest, weight).astype(BF16).reshape(2, half_tokens, width)

        def part(e):
            return first[ends.index(e)] if e in ends else block_of(rest, e)

        return Scatter(part, way)

    first_sums = ring_of(down_weight[:width], 1)
    second_sums = ring_of(down_weight[width:], -1)
    first_one = first_sums.step()
    second_one = second_sums.step()
    first_two = first_sums.step()
    second_two = second_sums.step(*first_one)
    up_theirs = to_y_hi(after(up_weight[:up_half], *second_one))
    first_three = first_sums.step(*second_one)
    second_three = second_sums.step(*first_two)
    up_more = to_y_hi(after(up_weight[up_half:], *first_two))
    first_sums.step(*second_two, up_theirs)
    second_sums.step(*first_three)

    slope = gelu_slope(after(pre_activation, *second_three).astype(F32))

    def grad_of(sums, slope):
        total = sums.result()
        mine = lax.dynamic_index_in_dim(total, y_hi, 0, keepdims=False)
        theirs = lax.dynamic_index_in_dim(total, 1 - y_hi, 0, keepdims=False)
        return (added(mine, to_y_hi(theirs.astype(BF16))) * slope).astype(BF16)

    first_grad = grad_of(first_sums, slope[:, :width])
    first_ring = Gather(first_grad, 1)
    second_ring = Gather(grad_of(second_sums, after(slope[:, width:], first_grad)), -1)

    up_theirs, up_more = after(up_theirs, *second_three), after(up_more, *second_three)
    up_all = jnp.concatenate([up_weight, up_theirs, up_more], axis=0)
    first_arrived = first_ring.step()
    late_cot = after(cotangent, *first_arrived)
    out_theirs = to_y_hi(after(out_weight, *first_arrived))
    out_all = jnp.concatenate([out_weight, out_theirs], axis=1)

    place = (core * 2 + y_lo) * N_X + x

    def rows_here(half):
        blocks = late_cot.reshape(2, N_Z, pieces, piece, feats)
        blocks = lax.dynamic_slice(
            blocks, (half, 0, place, 0, 0), (1, N_Z, 1, piece, feats)
        ).reshape(N_Z, piece, feats)
        blocks = lax.dynamic_slice_in_dim(jnp.concatenate([blocks, blocks], axis=0), z, N_Z, 0)
        return jnp.concatenate([blocks[e % N_Z] for e in ORDER], axis=0)

    cot_arrived = to_y_hi(rows_here(1 - y_hi))

    def block_products(group):
        left = [jnp.concatenate([first_ring.blocks[e], second_ring.blocks[e]], axis=1) for e in group]
        return times_transposed(jnp.concatenate(left, axis=0), up_all).astype(BF16)

    def in_pieces(product):
        count = product.shape[0] // rows
        product = product.reshape(count, pieces, piece, 2 * feats).transpose(1, 0, 2, 3)
        return product.reshape(pieces, count * piece, 2 * feats)

    def piece_sums(product):
        return lax.all_to_all(product, COLUMN, 0, 0, tiled=True)

    second_arrived = second_ring.step()
    first_second = first_ring.step()
    second_second = second_ring.step(*first_arrived)
    products = in_pieces(block_products(GROUPS[0]))
    sums = [piece_sums(products)]
    first_third = first_ring.step(*second_arrived)
    second_ring.step(*first_second, cot_arrived, products)
    first_ring.step(*second_second)
    second_ring.step(*first_third, out_theirs)
    products = [block_products(GROUPS[1][:4]), block_products(GROUPS[1][4:])]
    sums.append(piece_sums(after(in_pieces(jnp.concatenate(products, axis=0)), sums[0])))
    cot_here = jnp.concatenate([after(rows_here(y_hi), *second_arrived), cot_arrived], axis=1)
    totals, at = [], 0
    for arrived in sums:
        count = arrived.shape[1]
        part_sum = jnp.sum(arrived.astype(F32), axis=0) + cot_here[at:at + count].astype(F32)
        totals.append(part_sum.astype(BF16))
        at += count

    total = jnp.concatenate(totals, axis=0)
    copies = jnp.broadcast_to(total[None], (2 * N_X, *total.shape))
    own_pieces = lax.all_to_all(copies, ("y_lo", "x"), 0, 0, tiled=True)
    other_pieces = to_other_core(own_pieces)

    def out_products(whole):
        product = times_transposed(whole.reshape(half_tokens // 2, 2 * feats), out_all)
        return product.astype(BF16).reshape(2 * N_X, N_Z, piece, -1)

    own_product, other_product = out_products(own_pieces), out_products(other_pieces)

    def part(e):
        at = ORDER.index(4 if e == -4 else e)
        both = jnp.concatenate([own_product[:, at], other_product[:, at]], axis=0)
        return both.reshape(rows, -1)

    ring = Scatter(part, 1)
    for _ in range(4):
        ring.step()
    result = ring.result().astype(BF16)
    swapped = jnp.concatenate([result[rows // 2:], result[:rows // 2]], axis=0)
    return jnp.where(core == 0, result, swapped)


def solution(mesh):
    fine = Mesh(mesh.devices.reshape(2, 2, N_Z, 2, N_X), AXES)
    in_specs = (
        P(None, ROW),
        P(ROW, COLUMN),
        P(ROW, COLUMN),
        P(COLUMN, ROW),
        P(COLUMN, ROW),
    )
    return jax.shard_map(body, mesh=fine, in_specs=in_specs, out_specs=P(ROW, COLUMN), check_vma=False)
```

```python
import jax
import jax.numpy as jnp
from jax import lax
from jax.sharding import Mesh, PartitionSpec as P

N_Z = 8
N_X = 4
AXES = ("section", "y_hi", "z", "y_lo", "x")
ROW = ("y_hi", "z")
COLUMN = ("section", "y_lo", "x")
BF16 = jnp.bfloat16
F32 = jnp.float32
ORDER = (0, 1, -1, 2, -2, 3, -3, 4)
GROUPS = (ORDER[:3], ORDER[3:])


def gelu_slope(value):
    inner = 0.7978845608 * (value + 0.044715 * value * value * value)
    tanh_part = jnp.tanh(inner)
    derivative = 0.7978845608 * (1.0 + 3.0 * 0.044715 * value * value)
    return 0.5 * (1.0 + tanh_part) + 0.5 * value * (1.0 - tanh_part * tanh_part) * derivative


def times_transposed(left, right):
    return lax.dot_general(
        left, right, (((1,), (1,)), ((), ())), preferred_element_type=F32
    )


def move(value, where):
    pairs = []
    for core in range(2):
        for y_hi in range(2):
            for z in range(N_Z):
                for y_lo in range(2):
                    for x in range(N_X):
                        c, h, k, l, i = where(core, y_hi, z, y_lo, x)
                        source = ((core * 2 + y_hi) * N_Z + z) * 2 * N_X + y_lo * N_X + x
                        target = ((c * 2 + h) * N_Z + k % N_Z) * 2 * N_X + l * N_X + i % N_X
                        pairs.append((source, target))
    return lax.ppermute(value, AXES, pairs)


def to_y_hi(value):
    return move(value, lambda c, h, z, l, x: (c, 1 - h, z, l, x))


def to_other_core(value):
    return move(value, lambda c, h, z, l, x: (1 - c, h, z, l, x))


def along_z(value, sign):
    return move(value, lambda c, h, z, l, x: (c, h, z + sign, l, x))


def added(*terms):
    total = terms[0].astype(F32)
    for term in terms[1:]:
        total = total + term.astype(F32)
    return total


def after(value, *others):
    return lax.optimization_barrier((value, *others))[0]


class Scatter:
    def __init__(self, part, way):
        self.part, self.left, self.way = part, 4, way
        self.ahead = self.back = None

    def step(self, *waits):
        mine = self.part(self.way * self.left)
        far = self.part(self.way * (1 - self.left)) if self.left > 1 else None
        if self.ahead is not None:
            mine = added(mine, self.ahead)
            far = None if far is None else added(far, self.back)
        mine = mine.astype(BF16)
        if far is not None:
            mine, far = lax.optimization_barrier((mine, far.astype(BF16), *waits))[:2]
        elif waits:
            mine = after(mine, *waits)
        self.ahead = along_z(mine, self.way)
        if far is not None:
            self.back = along_z(far, -self.way)
        self.left -= 1
        return [self.ahead, self.back]

    def result(self):
        return added(self.part(0), self.ahead, self.back)


class Gather:
    def __init__(self, block, way):
        self.blocks, self.distance, self.way = {0: block}, 0, way
        self.ahead = self.back = block

    def step(self, *waits):
        self.distance += 1
        ahead, back = lax.optimization_barrier((self.ahead, self.back, *waits))[:2]
        self.ahead = along_z(ahead, self.way)
        self.blocks[4 if self.distance == 4 else -self.way * self.distance] = self.ahead
        if self.distance < 4:
            self.back = along_z(back, -self.way)
            self.blocks[self.way * self.distance] = self.back
        return [self.ahead, self.back]


def body(cotangent, pre_activation, up_weight, down_weight, out_weight):
    tokens, feats = cotangent.shape
    half_tokens = tokens // 2
    rows = half_tokens // N_Z
    pieces = 4 * N_X
    piece = rows // pieces
    core = lax.axis_index("section")
    y_hi = lax.axis_index("y_hi")
    z = lax.axis_index("z")
    y_lo = lax.axis_index("y_lo")
    x = lax.axis_index("x")

    def start_of(half, e):
        return half * half_tokens + ((z + e + N_Z) % N_Z) * rows

    def block_of(array, e):
        return lax.dynamic_slice_in_dim(array, start_of(0, e), rows, 1)

    width = down_weight.shape[0] // 2
    halves = cotangent.reshape(2, half_tokens, feats)

    quarters = cotangent.reshape(4, half_tokens // 2, feats)
    cot_sent = lax.dynamic_index_in_dim(quarters, (1 - y_hi) * 2 + core, 0, keepdims=False)
    cot_part = to_y_hi(cot_sent)
    down_theirs = to_y_hi(down_weight[width:])

    ends = (4, -3)
    ends_product = jnp.concatenate([block_of(halves, e) for e in ends], axis=0)
    ends_product = times_transposed(ends_product.reshape(4 * rows, feats), down_weight[:width]).astype(BF16)
    rest = times_transposed(after(cotangent, ends_product), down_weight[:width]).astype(BF16)
    rest = rest.reshape(2, half_tokens, width)

    def first_part(e):
        if e in ends:
            at = ends.index(e) * 2 * rows
            return ends_product[at:at + 2 * rows]
        return block_of(rest, e).reshape(2 * rows, width)

    first_sums = Scatter(first_part, 1)
    first_one = first_sums.step()
    first_two = first_sums.step()

    cot_part = after(cot_part, *first_one)
    cot_other = to_other_core(cot_part)
    down_theirs = after(down_theirs, *first_one)
    cot_theirs = jnp.concatenate(
        [jnp.where(core == 0, cot_part, cot_other), jnp.where(core == 0, cot_other, cot_part)], axis=0
    )
    cot_mine = lax.dynamic_index_in_dim(halves, y_hi, 0, keepdims=False)
    second_product = (
        times_transposed(cot_mine, down_weight[width:]) + times_transposed(cot_theirs, down_theirs)
    ).astype(BF16)
    second_sums = Scatter(
        lambda e: lax.dynamic_slice_in_dim(second_product, start_of(0, e), rows, 0), -1
    )
    first_three = first_sums.step()
    second_one = second_sums.step()
    first_four = first_sums.step(second_product)

    total = first_sums.result()
    first_mine = lax.dynamic_slice_in_dim(total, y_hi * rows, rows, 0)
    first_theirs = lax.dynamic_slice_in_dim(total, (1 - y_hi) * rows, rows, 0)
    first_theirs = to_y_hi(first_theirs.astype(BF16))
    second_two = second_sums.step(*first_three)
    slope = gelu_slope(after(pre_activation, *first_three).astype(F32))
    first_grad = (added(first_mine, first_theirs) * slope[:, :width]).astype(BF16)
    first_ring = Gather(first_grad, 1)
    first_arrived = first_ring.step()
    second_three = second_sums.step(*first_four)
    second_sums.step(*first_arrived)
    second_ring = Gather((second_sums.result() * slope[:, width:]).astype(BF16), -1)

    up_half = feats // 2
    up_theirs = to_y_hi(after(up_weight[:up_half], down_theirs))
    up_more = to_y_hi(after(up_weight[up_half:], first_theirs))
    up_theirs, up_more = after(up_theirs, *second_three), after(up_more, *second_three)
    up_all = jnp.concatenate([up_weight, up_theirs, up_more], axis=0)
    out_theirs = to_y_hi(after(out_weight, first_grad))
    out_all = jnp.concatenate([out_weight, out_theirs], axis=1)
    late_cot = after(cotangent, first_grad)

    place = (core * 2 + y_lo) * N_X + x

    def rows_here(half):
        blocks = late_cot.reshape(2, N_Z, pieces, piece, feats)
        blocks = lax.dynamic_slice(
            blocks, (half, 0, place, 0, 0), (1, N_Z, 1, piece, feats)
        ).reshape(N_Z, piece, feats)
        blocks = lax.dynamic_slice_in_dim(jnp.concatenate([blocks, blocks], axis=0), z, N_Z, 0)
        return jnp.concatenate([blocks[e % N_Z] for e in ORDER], axis=0)

    cot_arrived = to_y_hi(rows_here(1 - y_hi))

    def block_products(group):
        left = [jnp.concatenate([first_ring.blocks[e], second_ring.blocks[e]], axis=1) for e in group]
        return times_transposed(jnp.concatenate(left, axis=0), up_all).astype(BF16)

    def in_pieces(product):
        count = product.shape[0] // rows
        product = product.reshape(count, pieces, piece, 2 * feats).transpose(1, 0, 2, 3)
        return product.reshape(pieces, count * piece, 2 * feats)

    def piece_sums(product):
        return lax.all_to_all(product, COLUMN, 0, 0, tiled=True)

    second_arrived = second_ring.step()
    first_second = first_ring.step()
    second_second = second_ring.step(*first_arrived)
    products = in_pieces(block_products(GROUPS[0]))
    sums = [piece_sums(after(products, *second_second))]
    first_third = first_ring.step(*second_arrived)
    second_ring.step(*first_second, cot_arrived, products)
    first_ring.step(*second_second)
    second_ring.step(*first_third, out_theirs)
    products = [block_products(GROUPS[1][:4]), block_products(GROUPS[1][4:])]
    sums.append(piece_sums(after(in_pieces(jnp.concatenate(products, axis=0)), sums[0])))
    cot_here = jnp.concatenate([after(rows_here(y_hi), *second_arrived), cot_arrived], axis=1)
    totals, at = [], 0
    for arrived in sums:
        count = arrived.shape[1]
        part_sum = jnp.sum(arrived.astype(F32), axis=0) + cot_here[at:at + count].astype(F32)
        totals.append(part_sum.astype(BF16))
        at += count

    total = jnp.concatenate(totals, axis=0)
    copies = jnp.broadcast_to(total[None], (2 * N_X, *total.shape))
    own_pieces = lax.all_to_all(copies, ("y_lo", "x"), 0, 0, tiled=True)
    other_pieces = to_other_core(own_pieces)

    def out_products(whole):
        product = times_transposed(whole.reshape(half_tokens // 2, 2 * feats), out_all)
        return product.astype(BF16).reshape(2 * N_X, N_Z, piece, -1)

    own_product, other_product = out_products(own_pieces), out_products(other_pieces)

    def part(e):
        at = ORDER.index(4 if e == -4 else e)
        both = jnp.concatenate([own_product[:, at], other_product[:, at]], axis=0)
        return both.reshape(rows, -1)

    ring = Scatter(part, 1)
    for _ in range(4):
        ring.step()
    result = ring.result().astype(BF16)
    swapped = jnp.concatenate([result[rows // 2:], result[:rows // 2]], axis=0)
    return jnp.where(core == 0, result, swapped)


def solution(mesh):
    fine = Mesh(mesh.devices.reshape(2, 2, N_Z, 2, N_X), AXES)
    in_specs = (
        P(None, ROW),
        P(ROW, COLUMN),
        P(ROW, COLUMN),
        P(COLUMN, ROW),
        P(COLUMN, ROW),
    )
    return jax.shard_map(body, mesh=fine, in_specs=in_specs, out_specs=P(ROW, COLUMN), check_vma=False)
```

```python
import jax
import jax.numpy as jnp
from jax import lax
from jax.sharding import Mesh, PartitionSpec as P

N_Z = 8
N_X = 4
AXES = ("section", "y_hi", "z", "y_lo", "x")
ROW = ("y_hi", "z")
COLUMN = ("section", "y_lo", "x")
BF16 = jnp.bfloat16
F32 = jnp.float32
ORDER = (0, 1, -1, 2, -2, 3, -3, 4)
GROUPS = (ORDER[:3], ORDER[3:])


def gelu_slope(value):
    inner = 0.7978845608 * (value + 0.044715 * value * value * value)
    tanh_part = jnp.tanh(inner)
    derivative = 0.7978845608 * (1.0 + 3.0 * 0.044715 * value * value)
    return 0.5 * (1.0 + tanh_part) + 0.5 * value * (1.0 - tanh_part * tanh_part) * derivative


def times_transposed(left, right):
    return lax.dot_general(
        left, right, (((1,), (1,)), ((), ())), preferred_element_type=F32
    )


def move(value, where):
    pairs = []
    for core in range(2):
        for y_hi in range(2):
            for z in range(N_Z):
                for y_lo in range(2):
                    for x in range(N_X):
                        c, h, k, l, i = where(core, y_hi, z, y_lo, x)
                        source = ((core * 2 + y_hi) * N_Z + z) * 2 * N_X + y_lo * N_X + x
                        target = ((c * 2 + h) * N_Z + k % N_Z) * 2 * N_X + l * N_X + i % N_X
                        pairs.append((source, target))
    return lax.ppermute(value, AXES, pairs)


def to_y_hi(value):
    return move(value, lambda c, h, z, l, x: (c, 1 - h, z, l, x))


def to_other_core(value):
    return move(value, lambda c, h, z, l, x: (1 - c, h, z, l, x))


def along_z(value, sign):
    return move(value, lambda c, h, z, l, x: (c, h, z + sign, l, x))


def added(*terms):
    total = terms[0].astype(F32)
    for term in terms[1:]:
        total = total + term.astype(F32)
    return total


def after(value, *others):
    return lax.optimization_barrier((value, *others))[0]


class Scatter:
    def __init__(self, part, way):
        self.part, self.left, self.way = part, 4, way
        self.ahead = self.back = None

    def step(self, *waits):
        mine = self.part(self.way * self.left)
        far = self.part(self.way * (1 - self.left)) if self.left > 1 else None
        if self.ahead is not None:
            mine = added(mine, self.ahead)
            far = None if far is None else added(far, self.back)
        mine = mine.astype(BF16)
        if far is not None:
            mine, far = lax.optimization_barrier((mine, far.astype(BF16), *waits))[:2]
        elif waits:
            mine = after(mine, *waits)
        self.ahead = along_z(mine, self.way)
        if far is not None:
            self.back = along_z(far, -self.way)
        self.left -= 1
        return [self.ahead, self.back]

    def result(self):
        return added(self.part(0), self.ahead, self.back)


class Gather:
    def __init__(self, block, way):
        self.blocks, self.distance, self.way = {0: block}, 0, way
        self.ahead = self.back = block

    def step(self, *waits):
        self.distance += 1
        ahead, back = lax.optimization_barrier((self.ahead, self.back, *waits))[:2]
        self.ahead = along_z(ahead, self.way)
        self.blocks[4 if self.distance == 4 else -self.way * self.distance] = self.ahead
        if self.distance < 4:
            self.back = along_z(back, -self.way)
            self.blocks[self.way * self.distance] = self.back
        return [self.ahead, self.back]


def body(cotangent, pre_activation, up_weight, down_weight, out_weight):
    tokens, feats = cotangent.shape
    half_tokens = tokens // 2
    rows = half_tokens // N_Z
    pieces = 4 * N_X
    piece = rows // pieces
    core = lax.axis_index("section")
    y_hi = lax.axis_index("y_hi")
    z = lax.axis_index("z")
    y_lo = lax.axis_index("y_lo")
    x = lax.axis_index("x")

    def start_of(half, e):
        return half * half_tokens + ((z + e + N_Z) % N_Z) * rows

    def block_of(array, e):
        return lax.dynamic_slice_in_dim(array, start_of(0, e), rows, 1)

    width = down_weight.shape[0] // 2
    halves = cotangent.reshape(2, half_tokens, feats)

    quarters = cotangent.reshape(4, half_tokens // 2, feats)
    cot_sent = lax.dynamic_index_in_dim(quarters, (1 - y_hi) * 2 + core, 0, keepdims=False)
    cot_part = to_y_hi(cot_sent)
    down_theirs = to_y_hi(down_weight[width:])

    ends = (4, -3)
    ends_product = jnp.concatenate([block_of(halves, e) for e in ends], axis=0)
    ends_product = times_transposed(ends_product.reshape(4 * rows, feats), down_weight[:width]).astype(BF16)
    rest = times_transposed(after(cotangent, ends_product), down_weight[:width]).astype(BF16)
    rest = rest.reshape(2, half_tokens, width)

    def first_part(e):
        if e in ends:
            at = ends.index(e) * 2 * rows
            return ends_product[at:at + 2 * rows]
        return block_of(rest, e).reshape(2 * rows, width)

    first_sums = Scatter(first_part, 1)
    first_one = first_sums.step()
    first_two = first_sums.step()

    cot_part = after(cot_part, *first_one)
    cot_other = to_other_core(cot_part)
    down_theirs = after(down_theirs, *first_one)
    cot_theirs = jnp.concatenate(
        [jnp.where(core == 0, cot_part, cot_other), jnp.where(core == 0, cot_other, cot_part)], axis=0
    )
    cot_mine = lax.dynamic_index_in_dim(halves, y_hi, 0, keepdims=False)
    second_product = (
        times_transposed(cot_mine, down_weight[width:]) + times_transposed(cot_theirs, down_theirs)
    ).astype(BF16)
    second_sums = Scatter(
        lambda e: lax.dynamic_slice_in_dim(second_product, start_of(0, e), rows, 0), -1
    )
    first_three = first_sums.step()
    second_one = second_sums.step()
    first_four = first_sums.step(second_product)

    total = first_sums.result()
    first_mine = lax.dynamic_slice_in_dim(total, y_hi * rows, rows, 0)
    first_theirs = lax.dynamic_slice_in_dim(total, (1 - y_hi) * rows, rows, 0)
    first_theirs = to_y_hi(first_theirs.astype(BF16))
    out_theirs = to_y_hi(after(out_weight, down_theirs))
    second_two = second_sums.step(*first_three, out_theirs)
    slope = gelu_slope(after(pre_activation, *first_three).astype(F32))
    first_grad = (added(first_mine, first_theirs) * slope[:, :width]).astype(BF16)
    first_ring = Gather(first_grad, 1)
    first_arrived = first_ring.step()
    second_three = second_sums.step(*first_four)
    place = (core * 2 + y_lo) * N_X + x

    def rows_here(half):
        blocks = after(cotangent, *second_one).reshape(2, N_Z, pieces, piece, feats)
        blocks = lax.dynamic_slice(
            blocks, (half, 0, place, 0, 0), (1, N_Z, 1, piece, feats)
        ).reshape(N_Z, piece, feats)
        blocks = lax.dynamic_slice_in_dim(jnp.concatenate([blocks, blocks], axis=0), z, N_Z, 0)
        return jnp.concatenate([blocks[e % N_Z] for e in ORDER], axis=0)

    cot_arrived = to_y_hi(rows_here(1 - y_hi))

    second_sums.step(cot_arrived, first_grad)
    second_ring = Gather((second_sums.result() * after(slope[:, width:], first_grad)).astype(BF16), -1)

    up_half = feats // 2
    up_theirs = to_y_hi(after(up_weight[:up_half], down_theirs))
    up_more = to_y_hi(after(up_weight[up_half:], first_theirs))
    up_theirs, up_more = after(up_theirs, *second_three), after(up_more, *second_three)
    up_all = jnp.concatenate([up_weight, up_theirs, up_more], axis=0)
    out_all = jnp.concatenate([out_weight, out_theirs], axis=1)

    def block_products(group):
        left = [jnp.concatenate([first_ring.blocks[e], second_ring.blocks[e]], axis=1) for e in group]
        return times_transposed(jnp.concatenate(left, axis=0), up_all).astype(BF16)

    def in_pieces(product):
        count = product.shape[0] // rows
        product = product.reshape(count, pieces, piece, 2 * feats).transpose(1, 0, 2, 3)
        return product.reshape(pieces, count * piece, 2 * feats)

    def piece_sums(product):
        return lax.all_to_all(product, COLUMN, 0, 0, tiled=True)

    second_arrived = second_ring.step()
    first_second = first_ring.step()
    second_second = second_ring.step(*first_arrived)
    products = in_pieces(block_products(GROUPS[0]))
    sums = [piece_sums(after(products, *second_second))]
    first_third = first_ring.step(*second_arrived)
    second_ring.step(*first_second, products)
    first_ring.step(*second_second)
    second_ring.step(*first_third)
    products = [block_products(GROUPS[1][:4]), block_products(GROUPS[1][4:])]
    sums.append(piece_sums(after(in_pieces(jnp.concatenate(products, axis=0)), sums[0])))
    cot_here = jnp.concatenate([after(rows_here(y_hi), *second_arrived), cot_arrived], axis=1)
    totals, at = [], 0
    for arrived in sums:
        count = arrived.shape[1]
        part_sum = jnp.sum(arrived.astype(F32), axis=0) + cot_here[at:at + count].astype(F32)
        totals.append(part_sum.astype(BF16))
        at += count

    total = jnp.concatenate(totals, axis=0)
    copies = jnp.broadcast_to(total[None], (2 * N_X, *total.shape))
    own_pieces = lax.all_to_all(copies, ("y_lo", "x"), 0, 0, tiled=True)
    other_pieces = to_other_core(own_pieces)

    def out_products(whole):
        product = times_transposed(whole.reshape(half_tokens // 2, 2 * feats), out_all)
        return product.astype(BF16).reshape(2 * N_X, N_Z, piece, -1)

    own_product, other_product = out_products(own_pieces), out_products(other_pieces)

    def part(e):
        at = ORDER.index(4 if e == -4 else e)
        both = jnp.concatenate([own_product[:, at], other_product[:, at]], axis=0)
        return both.reshape(rows, -1)

    ring = Scatter(part, 1)
    for _ in range(4):
        ring.step()
    result = ring.result().astype(BF16)
    swapped = jnp.concatenate([result[rows // 2:], result[:rows // 2]], axis=0)
    return jnp.where(core == 0, result, swapped)


def solution(mesh):
    fine = Mesh(mesh.devices.reshape(2, 2, N_Z, 2, N_X), AXES)
    in_specs = (
        P(None, ROW),
        P(ROW, COLUMN),
        P(ROW, COLUMN),
        P(COLUMN, ROW),
        P(COLUMN, ROW),
    )
    return jax.shard_map(body, mesh=fine, in_specs=in_specs, out_specs=P(ROW, COLUMN), check_vma=False)
```

```python
import jax
import jax.numpy as jnp
from jax import lax
from jax.sharding import Mesh, PartitionSpec as P

N_Z = 8
N_X = 4
AXES = ("section", "y_hi", "z", "y_lo", "x")
ROW = ("y_hi", "z")
COLUMN = ("section", "y_lo", "x")
BF16 = jnp.bfloat16
F32 = jnp.float32
ORDER = (0, 1, -1, 2, -2, 3, -3, 4)
GROUPS = (ORDER[:3], ORDER[3:])


def gelu_slope(value):
    inner = 0.7978845608 * (value + 0.044715 * value * value * value)
    tanh_part = jnp.tanh(inner)
    derivative = 0.7978845608 * (1.0 + 3.0 * 0.044715 * value * value)
    return 0.5 * (1.0 + tanh_part) + 0.5 * value * (1.0 - tanh_part * tanh_part) * derivative


def times_transposed(left, right):
    return lax.dot_general(
        left, right, (((1,), (1,)), ((), ())), preferred_element_type=F32
    )


def move(value, where):
    pairs = []
    for core in range(2):
        for y_hi in range(2):
            for z in range(N_Z):
                for y_lo in range(2):
                    for x in range(N_X):
                        c, h, k, l, i = where(core, y_hi, z, y_lo, x)
                        source = ((core * 2 + y_hi) * N_Z + z) * 2 * N_X + y_lo * N_X + x
                        target = ((c * 2 + h) * N_Z + k % N_Z) * 2 * N_X + l * N_X + i % N_X
                        pairs.append((source, target))
    return lax.ppermute(value, AXES, pairs)


def to_y_hi(value):
    return move(value, lambda c, h, z, l, x: (c, 1 - h, z, l, x))


def to_other_core(value):
    return move(value, lambda c, h, z, l, x: (1 - c, h, z, l, x))


def along_z(value, sign):
    return move(value, lambda c, h, z, l, x: (c, h, z + sign, l, x))


def added(*terms):
    total = terms[0].astype(F32)
    for term in terms[1:]:
        total = total + term.astype(F32)
    return total


def after(value, *others):
    return lax.optimization_barrier((value, *others))[0]


class Scatter:
    def __init__(self, part, way):
        self.part, self.left, self.way = part, 4, way
        self.ahead = self.back = None

    def step(self, *waits):
        mine = self.part(self.way * self.left)
        far = self.part(self.way * (1 - self.left)) if self.left > 1 else None
        if self.ahead is not None:
            mine = added(mine, self.ahead)
            far = None if far is None else added(far, self.back)
        mine = mine.astype(BF16)
        if far is not None:
            mine, far = lax.optimization_barrier((mine, far.astype(BF16), *waits))[:2]
        elif waits:
            mine = after(mine, *waits)
        self.ahead = along_z(mine, self.way)
        if far is not None:
            self.back = along_z(far, -self.way)
        self.left -= 1
        return [self.ahead, self.back]

    def result(self):
        return added(self.part(0), self.ahead, self.back)


class Gather:
    def __init__(self, block, way):
        self.blocks, self.distance, self.way = {0: block}, 0, way
        self.ahead = self.back = block

    def step(self, *waits):
        self.distance += 1
        ahead, back = lax.optimization_barrier((self.ahead, self.back, *waits))[:2]
        self.ahead = along_z(ahead, self.way)
        self.blocks[4 if self.distance == 4 else -self.way * self.distance] = self.ahead
        if self.distance < 4:
            self.back = along_z(back, -self.way)
            self.blocks[self.way * self.distance] = self.back
        return [self.ahead, self.back]


def body(cotangent, pre_activation, up_weight, down_weight, out_weight):
    tokens, feats = cotangent.shape
    half_tokens = tokens // 2
    rows = half_tokens // N_Z
    pieces = 4 * N_X
    piece = rows // pieces
    core = lax.axis_index("section")
    y_hi = lax.axis_index("y_hi")
    z = lax.axis_index("z")
    y_lo = lax.axis_index("y_lo")
    x = lax.axis_index("x")

    def start_of(half, e):
        return half * half_tokens + ((z + e + N_Z) % N_Z) * rows

    def block_of(array, e):
        return lax.dynamic_slice_in_dim(array, start_of(0, e), rows, 1)

    width = down_weight.shape[0] // 2
    halves = cotangent.reshape(2, half_tokens, feats)

    quarters = cotangent.reshape(4, half_tokens // 2, feats)
    cot_sent = lax.dynamic_index_in_dim(quarters, (1 - y_hi) * 2 + core, 0, keepdims=False)
    cot_part = to_y_hi(cot_sent)
    down_theirs = to_y_hi(down_weight[width:])

    ends = (4, -3)
    ends_product = jnp.concatenate([block_of(halves, e) for e in ends], axis=0)
    ends_product = times_transposed(ends_product.reshape(4 * rows, feats), down_weight[:width]).astype(BF16)
    rest = times_transposed(after(cotangent, ends_product), down_weight[:width]).astype(BF16)
    rest = rest.reshape(2, half_tokens, width)

    def first_part(e):
        if e in ends:
            at = ends.index(e) * 2 * rows
            return ends_product[at:at + 2 * rows]
        return block_of(rest, e).reshape(2 * rows, width)

    first_sums = Scatter(first_part, 1)
    first_one = first_sums.step()
    first_two = first_sums.step()

    cot_part = after(cot_part, *first_one)
    cot_other = to_other_core(cot_part)
    down_theirs = after(down_theirs, *first_one)
    cot_theirs = jnp.concatenate(
        [jnp.where(core == 0, cot_part, cot_other), jnp.where(core == 0, cot_other, cot_part)], axis=0
    )
    cot_mine = lax.dynamic_index_in_dim(after(halves, *first_one), y_hi, 0, keepdims=False)
    second_product = (
        times_transposed(cot_mine, down_weight[width:]) + times_transposed(cot_theirs, down_theirs)
    ).astype(BF16)
    second_sums = Scatter(
        lambda e: lax.dynamic_slice_in_dim(second_product, start_of(0, e), rows, 0), -1
    )
    first_three = first_sums.step()
    second_one = second_sums.step()
    first_four = first_sums.step(second_product)

    total = first_sums.result()
    first_mine = lax.dynamic_slice_in_dim(total, y_hi * rows, rows, 0)
    first_theirs = lax.dynamic_slice_in_dim(total, (1 - y_hi) * rows, rows, 0)
    first_theirs = to_y_hi(first_theirs.astype(BF16))
    out_theirs = to_y_hi(after(out_weight, *second_one))
    second_two = second_sums.step(*first_three)
    slope = gelu_slope(after(pre_activation, *first_three).astype(F32))
    first_grad = (added(first_mine, first_theirs) * slope[:, :width]).astype(BF16)
    first_ring = Gather(first_grad, 1)
    first_arrived = first_ring.step()
    second_three = second_sums.step(*first_four)
    place = (core * 2 + y_lo) * N_X + x

    def rows_here(half):
        blocks = after(cotangent, *second_two).reshape(2, N_Z, pieces, piece, feats)
        blocks = lax.dynamic_slice(
            blocks, (half, 0, place, 0, 0), (1, N_Z, 1, piece, feats)
        ).reshape(N_Z, piece, feats)
        blocks = lax.dynamic_slice_in_dim(jnp.concatenate([blocks, blocks], axis=0), z, N_Z, 0)
        return jnp.concatenate([blocks[e % N_Z] for e in ORDER], axis=0)

    cot_arrived = to_y_hi(rows_here(1 - y_hi))

    second_sums.step(first_grad, out_theirs)
    second_ring = Gather((second_sums.result() * after(slope[:, width:], first_grad)).astype(BF16), -1)

    up_half = feats // 2
    up_theirs = to_y_hi(after(up_weight[:up_half], down_theirs))
    up_more = to_y_hi(after(up_weight[up_half:], first_theirs))
    up_theirs, up_more = after(up_theirs, *second_three), after(up_more, *second_three)
    up_all = jnp.concatenate([up_weight, up_theirs, up_more], axis=0)
    out_all = jnp.concatenate([out_weight, out_theirs], axis=1)

    def block_products(group):
        left = [jnp.concatenate([first_ring.blocks[e], second_ring.blocks[e]], axis=1) for e in group]
        return times_transposed(jnp.concatenate(left, axis=0), up_all).astype(BF16)

    def in_pieces(product):
        count = product.shape[0] // rows
        product = product.reshape(count, pieces, piece, 2 * feats).transpose(1, 0, 2, 3)
        return product.reshape(pieces, count * piece, 2 * feats)

    def piece_sums(product):
        return lax.all_to_all(product, COLUMN, 0, 0, tiled=True)

    second_arrived = second_ring.step()
    first_second = first_ring.step()
    second_second = second_ring.step(*first_arrived, cot_arrived)
    products = in_pieces(block_products(GROUPS[0]))
    sums = [piece_sums(after(products, *second_second))]
    first_third = first_ring.step(*second_arrived)
    second_ring.step(*first_second, products)
    first_ring.step(*second_second)
    second_ring.step(*first_third)
    products = [block_products(GROUPS[1][:4]), block_products(GROUPS[1][4:])]
    sums.append(piece_sums(after(in_pieces(jnp.concatenate(products, axis=0)), sums[0])))
    cot_here = jnp.concatenate([after(rows_here(y_hi), *second_arrived), cot_arrived], axis=1)
    totals, at = [], 0
    for arrived in sums:
        count = arrived.shape[1]
        part_sum = jnp.sum(arrived.astype(F32), axis=0) + cot_here[at:at + count].astype(F32)
        totals.append(part_sum.astype(BF16))
        at += count

    total = jnp.concatenate(totals, axis=0)
    copies = jnp.broadcast_to(total[None], (2 * N_X, *total.shape))
    own_pieces = lax.all_to_all(copies, ("y_lo", "x"), 0, 0, tiled=True)
    other_pieces = to_other_core(own_pieces)

    def out_products(whole):
        product = times_transposed(whole.reshape(half_tokens // 2, 2 * feats), out_all)
        return product.astype(BF16).reshape(2 * N_X, N_Z, piece, -1)

    own_product, other_product = out_products(own_pieces), out_products(other_pieces)

    def part(e):
        at = ORDER.index(4 if e == -4 else e)
        both = jnp.concatenate([own_product[:, at], other_product[:, at]], axis=0)
        return both.reshape(rows, -1)

    ring = Scatter(part, 1)
    for _ in range(4):
        ring.step()
    result = ring.result().astype(BF16)
    swapped = jnp.concatenate([result[rows // 2:], result[:rows // 2]], axis=0)
    return jnp.where(core == 0, result, swapped)


def solution(mesh):
    fine = Mesh(mesh.devices.reshape(2, 2, N_Z, 2, N_X), AXES)
    in_specs = (
        P(None, ROW),
        P(ROW, COLUMN),
        P(ROW, COLUMN),
        P(COLUMN, ROW),
        P(COLUMN, ROW),
    )
    return jax.shard_map(body, mesh=fine, in_specs=in_specs, out_specs=P(ROW, COLUMN), check_vma=False)
```

```python
import jax
import jax.numpy as jnp
from jax import lax
from jax.sharding import Mesh, PartitionSpec as P

N_Z = 8
N_X = 4
AXES = ("section", "y_hi", "z", "y_lo", "x")
ROW = ("y_hi", "z")
COLUMN = ("section", "y_lo", "x")
BF16 = jnp.bfloat16
F32 = jnp.float32
ORDER = (0, 1, -1, 2, -2, 3, -3, 4)
GROUPS = (ORDER[:3], ORDER[3:])


def gelu_slope(value):
    inner = 0.7978845608 * (value + 0.044715 * value * value * value)
    tanh_part = jnp.tanh(inner)
    derivative = 0.7978845608 * (1.0 + 3.0 * 0.044715 * value * value)
    return 0.5 * (1.0 + tanh_part) + 0.5 * value * (1.0 - tanh_part * tanh_part) * derivative


def times_transposed(left, right):
    return lax.dot_general(
        left, right, (((1,), (1,)), ((), ())), preferred_element_type=F32
    )


def move(value, where):
    pairs = []
    for core in range(2):
        for y_hi in range(2):
            for z in range(N_Z):
                for y_lo in range(2):
                    for x in range(N_X):
                        c, h, k, l, i = where(core, y_hi, z, y_lo, x)
                        source = ((core * 2 + y_hi) * N_Z + z) * 2 * N_X + y_lo * N_X + x
                        target = ((c * 2 + h) * N_Z + k % N_Z) * 2 * N_X + l * N_X + i % N_X
                        pairs.append((source, target))
    return lax.ppermute(value, AXES, pairs)


def to_y_hi(value):
    return move(value, lambda c, h, z, l, x: (c, 1 - h, z, l, x))


def to_other_core(value):
    return move(value, lambda c, h, z, l, x: (1 - c, h, z, l, x))


def along_z(value, sign):
    return move(value, lambda c, h, z, l, x: (c, h, z + sign, l, x))


def added(*terms):
    total = terms[0].astype(F32)
    for term in terms[1:]:
        total = total + term.astype(F32)
    return total


def after(value, *others):
    return lax.optimization_barrier((value, *others))[0]


class Scatter:
    def __init__(self, part, way):
        self.part, self.left, self.way = part, 4, way
        self.ahead = self.back = None

    def step(self, *waits):
        mine = self.part(self.way * self.left)
        far = self.part(self.way * (1 - self.left)) if self.left > 1 else None
        if self.ahead is not None:
            mine = added(mine, self.ahead)
            far = None if far is None else added(far, self.back)
        mine = mine.astype(BF16)
        if far is not None:
            mine, far = lax.optimization_barrier((mine, far.astype(BF16), *waits))[:2]
        elif waits:
            mine = after(mine, *waits)
        self.ahead = along_z(mine, self.way)
        if far is not None:
            self.back = along_z(far, -self.way)
        self.left -= 1
        return [self.ahead, self.back]

    def result(self):
        return added(self.part(0), self.ahead, self.back)


class Gather:
    def __init__(self, block, way):
        self.blocks, self.distance, self.way = {0: block}, 0, way
        self.ahead = self.back = block

    def step(self, *waits):
        self.distance += 1
        ahead, back = lax.optimization_barrier((self.ahead, self.back, *waits))[:2]
        self.ahead = along_z(ahead, self.way)
        self.blocks[4 if self.distance == 4 else -self.way * self.distance] = self.ahead
        if self.distance < 4:
            self.back = along_z(back, -self.way)
            self.blocks[self.way * self.distance] = self.back
        return [self.ahead, self.back]


def body(cotangent, pre_activation, up_weight, down_weight, out_weight):
    tokens, feats = cotangent.shape
    half_tokens = tokens // 2
    rows = half_tokens // N_Z
    pieces = 4 * N_X
    piece = rows // pieces
    core = lax.axis_index("section")
    y_hi = lax.axis_index("y_hi")
    z = lax.axis_index("z")
    y_lo = lax.axis_index("y_lo")
    x = lax.axis_index("x")

    def start_of(half, e):
        return half * half_tokens + ((z + e + N_Z) % N_Z) * rows

    def block_of(array, e):
        return lax.dynamic_slice_in_dim(array, start_of(0, e), rows, 1)

    width = down_weight.shape[0] // 2
    halves = cotangent.reshape(2, half_tokens, feats)

    quarters = cotangent.reshape(4, half_tokens // 2, feats)
    cot_sent = lax.dynamic_index_in_dim(quarters, (1 - y_hi) * 2 + core, 0, keepdims=False)
    cot_part = to_y_hi(cot_sent)
    down_theirs = to_y_hi(down_weight[width:])

    ends = (4, -3)
    ends_product = jnp.concatenate([block_of(halves, e) for e in ends], axis=0)
    ends_product = times_transposed(ends_product.reshape(4 * rows, feats), down_weight[:width]).astype(BF16)
    rest = times_transposed(after(cotangent, ends_product), down_weight[:width]).astype(BF16)
    rest = rest.reshape(2, half_tokens, width)

    def first_part(e):
        if e in ends:
            at = ends.index(e) * 2 * rows
            return ends_product[at:at + 2 * rows]
        return block_of(rest, e).reshape(2 * rows, width)

    first_sums = Scatter(first_part, 1)
    first_one = first_sums.step()
    first_two = first_sums.step()

    cot_part = after(cot_part, *first_one)
    cot_other = to_other_core(cot_part)
    down_theirs = after(down_theirs, *first_one)
    cot_theirs = jnp.concatenate(
        [jnp.where(core == 0, cot_part, cot_other), jnp.where(core == 0, cot_other, cot_part)], axis=0
    )
    cot_mine = lax.dynamic_index_in_dim(after(halves, *first_one), y_hi, 0, keepdims=False)
    second_product = (
        times_transposed(cot_mine, down_weight[width:]) + times_transposed(cot_theirs, down_theirs)
    ).astype(BF16)
    second_sums = Scatter(
        lambda e: lax.dynamic_slice_in_dim(second_product, start_of(0, e), rows, 0), -1
    )
    first_three = first_sums.step()
    second_one = second_sums.step()
    first_four = first_sums.step(second_product)

    total = first_sums.result()
    first_mine = lax.dynamic_slice_in_dim(total, y_hi * rows, rows, 0)
    first_theirs = lax.dynamic_slice_in_dim(total, (1 - y_hi) * rows, rows, 0)
    first_theirs = to_y_hi(first_theirs.astype(BF16))
    out_theirs = to_y_hi(after(out_weight, *second_one))
    second_two = second_sums.step(*first_three)
    slope = gelu_slope(after(pre_activation, *first_three).astype(F32))
    first_grad = (added(first_mine, first_theirs) * slope[:, :width]).astype(BF16)
    first_ring = Gather(first_grad, 1)
    first_arrived = first_ring.step()
    second_three = second_sums.step(*first_four)
    place = (core * 2 + y_lo) * N_X + x

    def rows_here(half):
        blocks = after(cotangent, *second_two).reshape(2, N_Z, pieces, piece, feats)
        blocks = lax.dynamic_slice(
            blocks, (half, 0, place, 0, 0), (1, N_Z, 1, piece, feats)
        ).reshape(N_Z, piece, feats)
        blocks = lax.dynamic_slice_in_dim(jnp.concatenate([blocks, blocks], axis=0), z, N_Z, 0)
        return jnp.concatenate([blocks[e % N_Z] for e in ORDER], axis=0)

    cot_arrived = to_y_hi(rows_here(1 - y_hi))

    second_sums.step(first_grad, out_theirs)
    second_ring = Gather((second_sums.result() * after(slope[:, width:], first_grad)).astype(BF16), -1)

    up_half = feats // 2
    up_theirs = to_y_hi(after(up_weight[:up_half], down_theirs))
    up_more = to_y_hi(after(up_weight[up_half:], first_theirs, cot_arrived))
    up_theirs, up_more = after(up_theirs, *second_three), after(up_more, *second_three)
    up_all = jnp.concatenate([up_weight, up_theirs, up_more], axis=0)
    out_all = jnp.concatenate([out_weight, out_theirs], axis=1)

    def block_products(group):
        left = [jnp.concatenate([first_ring.blocks[e], second_ring.blocks[e]], axis=1) for e in group]
        return times_transposed(jnp.concatenate(left, axis=0), up_all).astype(BF16)

    def in_pieces(product):
        count = product.shape[0] // rows
        product = product.reshape(count, pieces, piece, 2 * feats).transpose(1, 0, 2, 3)
        return product.reshape(pieces, count * piece, 2 * feats)

    def piece_sums(product):
        return lax.all_to_all(product, COLUMN, 0, 0, tiled=True)

    second_arrived = second_ring.step()
    first_second = first_ring.step()
    second_second = second_ring.step(*first_arrived, cot_arrived)
    products = in_pieces(block_products(GROUPS[0]))
    sums = [piece_sums(after(products, *second_second))]
    first_third = first_ring.step(*second_arrived)
    second_ring.step(*first_second, products)
    first_ring.step(*second_second)
    second_ring.step(*first_third)
    products = [block_products(GROUPS[1][:4]), block_products(GROUPS[1][4:])]
    sums.append(piece_sums(after(in_pieces(jnp.concatenate(products, axis=0)), sums[0])))
    cot_here = jnp.concatenate([after(rows_here(y_hi), *second_arrived), cot_arrived], axis=1)
    totals, at = [], 0
    for arrived in sums:
        count = arrived.shape[1]
        part_sum = jnp.sum(arrived.astype(F32), axis=0) + cot_here[at:at + count].astype(F32)
        totals.append(part_sum.astype(BF16))
        at += count

    total = jnp.concatenate(totals, axis=0)
    copies = jnp.broadcast_to(total[None], (2 * N_X, *total.shape))
    own_pieces = lax.all_to_all(copies, ("y_lo", "x"), 0, 0, tiled=True)
    other_pieces = to_other_core(own_pieces)

    def out_products(whole):
        product = times_transposed(whole.reshape(half_tokens // 2, 2 * feats), out_all)
        return product.astype(BF16).reshape(2 * N_X, N_Z, piece, -1)

    own_product, other_product = out_products(own_pieces), out_products(other_pieces)

    def part(e):
        at = ORDER.index(4 if e == -4 else e)
        both = jnp.concatenate([own_product[:, at], other_product[:, at]], axis=0)
        return both.reshape(rows, -1)

    ring = Scatter(part, 1)
    for _ in range(4):
        ring.step()
    result = ring.result().astype(BF16)
    swapped = jnp.concatenate([result[rows // 2:], result[:rows // 2]], axis=0)
    return jnp.where(core == 0, result, swapped)


def solution(mesh):
    fine = Mesh(mesh.devices.reshape(2, 2, N_Z, 2, N_X), AXES)
    in_specs = (
        P(None, ROW),
        P(ROW, COLUMN),
        P(ROW, COLUMN),
        P(COLUMN, ROW),
        P(COLUMN, ROW),
    )
    return jax.shard_map(body, mesh=fine, in_specs=in_specs, out_specs=P(ROW, COLUMN), check_vma=False)
```

```python
import jax
import jax.numpy as jnp
from jax import lax
from jax.sharding import Mesh, PartitionSpec as P

N_Z = 8
N_X = 4
AXES = ("section", "y_hi", "z", "y_lo", "x")
ROW = ("y_hi", "z")
COLUMN = ("section", "y_lo", "x")
BF16 = jnp.bfloat16
F32 = jnp.float32
ORDER = (0, 1, -1, 2, -2, 3, -3, 4)
GROUPS = (ORDER[:3], ORDER[3:])


def gelu_slope(value):
    inner = 0.7978845608 * (value + 0.044715 * value * value * value)
    tanh_part = jnp.tanh(inner)
    derivative = 0.7978845608 * (1.0 + 3.0 * 0.044715 * value * value)
    return 0.5 * (1.0 + tanh_part) + 0.5 * value * (1.0 - tanh_part * tanh_part) * derivative


def times_transposed(left, right):
    return lax.dot_general(
        left, right, (((1,), (1,)), ((), ())), preferred_element_type=F32
    )


def move(value, where):
    pairs = []
    for core in range(2):
        for y_hi in range(2):
            for z in range(N_Z):
                for y_lo in range(2):
                    for x in range(N_X):
                        c, h, k, l, i = where(core, y_hi, z, y_lo, x)
                        source = ((core * 2 + y_hi) * N_Z + z) * 2 * N_X + y_lo * N_X + x
                        target = ((c * 2 + h) * N_Z + k % N_Z) * 2 * N_X + l * N_X + i % N_X
                        pairs.append((source, target))
    return lax.ppermute(value, AXES, pairs)


def to_y_hi(value):
    return move(value, lambda c, h, z, l, x: (c, 1 - h, z, l, x))


def to_other_core(value):
    return move(value, lambda c, h, z, l, x: (1 - c, h, z, l, x))


def along_z(value, sign):
    return move(value, lambda c, h, z, l, x: (c, h, z + sign, l, x))


def added(*terms):
    total = terms[0].astype(F32)
    for term in terms[1:]:
        total = total + term.astype(F32)
    return total


def after(value, *others):
    return lax.optimization_barrier((value, *others))[0]


class Scatter:
    def __init__(self, part, way):
        self.part, self.left, self.way = part, 4, way
        self.ahead = self.back = None

    def step(self, *waits):
        mine = self.part(self.way * self.left)
        far = self.part(self.way * (1 - self.left)) if self.left > 1 else None
        if self.ahead is not None:
            mine = added(mine, self.ahead)
            far = None if far is None else added(far, self.back)
        mine = mine.astype(BF16)
        if far is not None:
            mine, far = lax.optimization_barrier((mine, far.astype(BF16), *waits))[:2]
        elif waits:
            mine = after(mine, *waits)
        self.ahead = along_z(mine, self.way)
        if far is not None:
            self.back = along_z(far, -self.way)
        self.left -= 1
        return [self.ahead, self.back]

    def result(self):
        return added(self.part(0), self.ahead, self.back)


class Gather:
    def __init__(self, block, way):
        self.blocks, self.distance, self.way = {0: block}, 0, way
        self.ahead = self.back = block

    def step(self, *waits):
        self.distance += 1
        ahead, back = lax.optimization_barrier((self.ahead, self.back, *waits))[:2]
        self.ahead = along_z(ahead, self.way)
        self.blocks[4 if self.distance == 4 else -self.way * self.distance] = self.ahead
        if self.distance < 4:
            self.back = along_z(back, -self.way)
            self.blocks[self.way * self.distance] = self.back
        return [self.ahead, self.back]


def body(cotangent, pre_activation, up_weight, down_weight, out_weight):
    tokens, feats = cotangent.shape
    half_tokens = tokens // 2
    rows = half_tokens // N_Z
    pieces = 4 * N_X
    piece = rows // pieces
    core = lax.axis_index("section")
    y_hi = lax.axis_index("y_hi")
    z = lax.axis_index("z")
    y_lo = lax.axis_index("y_lo")
    x = lax.axis_index("x")

    def start_of(half, e):
        return half * half_tokens + ((z + e + N_Z) % N_Z) * rows

    def block_of(array, e):
        return lax.dynamic_slice_in_dim(array, start_of(0, e), rows, 1)

    up_half = feats // 2
    up_theirs = to_y_hi(up_weight[:up_half])

    width = down_weight.shape[0] // 2
    halves = cotangent.reshape(2, half_tokens, feats)

    def ring_of(weight, way):
        ends = (4 * way, -3 * way)
        first = jnp.concatenate([block_of(halves, e) for e in ends], axis=0)
        first = times_transposed(first.reshape(4 * rows, feats), weight).astype(BF16)
        first = first.reshape(2, 2, rows, width)
        rest = after(cotangent, first)
        rest = times_transposed(rest, weight).astype(BF16).reshape(2, half_tokens, width)

        def part(e):
            return first[ends.index(e)] if e in ends else block_of(rest, e)

        return Scatter(part, way)

    first_sums = ring_of(down_weight[:width], 1)
    second_sums = ring_of(down_weight[width:], -1)
    first_one = first_sums.step()
    second_one = second_sums.step()
    first_two = first_sums.step()
    second_two = second_sums.step(*first_one)
    up_more = to_y_hi(after(up_weight[up_half:], *first_one))
    first_three = first_sums.step(*second_one, up_theirs)
    second_three = second_sums.step(*first_two)
    out_theirs = to_y_hi(after(out_weight, *first_two))
    first_sums.step(*second_two, up_more)
    second_sums.step(*first_three, out_theirs)

    slope = gelu_slope(after(pre_activation, *second_three).astype(F32))

    def grad_of(sums, slope):
        total = sums.result()
        mine = lax.dynamic_index_in_dim(total, y_hi, 0, keepdims=False)
        theirs = lax.dynamic_index_in_dim(total, 1 - y_hi, 0, keepdims=False)
        return (added(mine, to_y_hi(theirs.astype(BF16))) * slope).astype(BF16)

    first_grad = grad_of(first_sums, slope[:, :width])
    first_ring = Gather(first_grad, 1)
    second_ring = Gather(grad_of(second_sums, after(slope[:, width:], first_grad)), -1)

    up_theirs, up_more = after(up_theirs, *second_three), after(up_more, *second_three)
    up_all = jnp.concatenate([up_weight, up_theirs, up_more], axis=0)
    first_arrived = first_ring.step()
    late_cot = after(cotangent, *first_arrived)
    out_all = jnp.concatenate([out_weight, out_theirs], axis=1)

    place = (core * 2 + y_lo) * N_X + x

    def rows_here(half):
        blocks = late_cot.reshape(2, N_Z, pieces, piece, feats)
        blocks = lax.dynamic_slice(
            blocks, (half, 0, place, 0, 0), (1, N_Z, 1, piece, feats)
        ).reshape(N_Z, piece, feats)
        blocks = lax.dynamic_slice_in_dim(jnp.concatenate([blocks, blocks], axis=0), z, N_Z, 0)
        return jnp.concatenate([blocks[e % N_Z] for e in ORDER], axis=0)

    cot_arrived = to_y_hi(rows_here(1 - y_hi))

    def block_products(group):
        left = [jnp.concatenate([first_ring.blocks[e], second_ring.blocks[e]], axis=1) for e in group]
        return times_transposed(jnp.concatenate(left, axis=0), up_all).astype(BF16)

    def in_pieces(product):
        count = product.shape[0] // rows
        product = product.reshape(count, pieces, piece, 2 * feats).transpose(1, 0, 2, 3)
        return product.reshape(pieces, count * piece, 2 * feats)

    def piece_sums(product):
        return lax.all_to_all(product, COLUMN, 0, 0, tiled=True)

    second_arrived = second_ring.step()
    first_second = first_ring.step()
    second_second = second_ring.step(*first_arrived)
    products = in_pieces(block_products(GROUPS[0]))
    sums = [piece_sums(after(products, *second_second))]
    first_third = first_ring.step(*second_arrived)
    second_ring.step(*first_second, cot_arrived, products)
    first_ring.step(*second_second)
    second_ring.step(*first_third)
    products = [block_products(GROUPS[1][:4]), block_products(GROUPS[1][4:])]
    sums.append(piece_sums(after(in_pieces(jnp.concatenate(products, axis=0)), sums[0])))
    cot_here = jnp.concatenate([after(rows_here(y_hi), *second_arrived), cot_arrived], axis=1)
    totals, at = [], 0
    for arrived in sums:
        count = arrived.shape[1]
        part_sum = jnp.sum(arrived.astype(F32), axis=0) + cot_here[at:at + count].astype(F32)
        totals.append(part_sum.astype(BF16))
        at += count

    total = jnp.concatenate(totals, axis=0)
    copies = jnp.broadcast_to(total[None], (2 * N_X, *total.shape))
    own_pieces = lax.all_to_all(copies, ("y_lo", "x"), 0, 0, tiled=True)
    other_pieces = to_other_core(own_pieces)

    def out_products(whole):
        product = times_transposed(whole.reshape(half_tokens // 2, 2 * feats), out_all)
        return product.astype(BF16).reshape(2 * N_X, N_Z, piece, -1)

    own_product, other_product = out_products(own_pieces), out_products(other_pieces)

    def part(e):
        at = ORDER.index(4 if e == -4 else e)
        both = jnp.concatenate([own_product[:, at], other_product[:, at]], axis=0)
        return both.reshape(rows, -1)

    ring = Scatter(part, 1)
    for _ in range(4):
        ring.step()
    result = ring.result().astype(BF16)
    swapped = jnp.concatenate([result[rows // 2:], result[:rows // 2]], axis=0)
    return jnp.where(core == 0, result, swapped)


def solution(mesh):
    fine = Mesh(mesh.devices.reshape(2, 2, N_Z, 2, N_X), AXES)
    in_specs = (
        P(None, ROW),
        P(ROW, COLUMN),
        P(ROW, COLUMN),
        P(COLUMN, ROW),
        P(COLUMN, ROW),
    )
    return jax.shard_map(body, mesh=fine, in_specs=in_specs, out_specs=P(ROW, COLUMN), check_vma=False)
```
